512 devices in a mesh: seq: 64 (over y, z), dp: 8 (over x, core).
Axes of the slice: x: 4, y: 4, z: 16, core: 2. Of those that a mesh axis runs over, the one named last changes fastest.
Arguments:
- queries: bfloat16 [8, 512, 4096], P('dp', 'seq'), may hold values from -8 to 8
- key_vectors: bfloat16 [8, 8192, 4096], P('dp', 'seq'), may hold values from -6 to 6
- value_vectors: bfloat16 [8, 8192, 4096], P('dp', 'seq'), may hold values from -6 to 6
- saved_out: bfloat16 [8, 512, 4096], P('dp', 'seq'), may hold values from -6 to 6
- grad_out: bfloat16 [8, 512, 4096], P('dp', 'seq'), may hold values from -192 to 192
- out_weight: bfloat16 [4096, 4096], P('seq', 'dp'), may hold values from -0.09375 to 0.09375
- window_start: int32 [8], P('dp'), may hold values from 1 to 7680
- block_order: int32 [64], replicated, may hold values from 0 to 63, each once
Outputs:
- grad_queries: bfloat16 [8, 512, 4096], P('dp', 'seq')
- grad_keys: bfloat16 [8, 8192, 4096], P('dp', 'seq')
- grad_values: bfloat16 [8, 8192, 4096], P('dp', 'seq')
- grad_weight: float32 [4096, 4096], P('seq', 'dp')
The draws below stay inside these ranges and needn't reach their ends.
Inputs may be any that keep to these rules, and one draw needn't show every extreme that they name: `block_order`: a permutation of the 64 query blocks. `window_start`: the window's last query lies inside the prefix.
All inputs are finite; a program needn't handle non-finite values.
Results may differ from the reference program's by a relative error of at most 0.017.
Values may be sent and summed in bfloat16 or wider, within the bound.
A program may use at most 64 MiB of HBM per device.

```python
import math
import jax
import jax.numpy as jnp
from jax import lax

H = 32
HD = 128
D = 4096
Q_DEV = 8
KV_DEV = 128
QW = 512
L = 8192
SEQS = 8
N_SEQ = 64


def draw_queries(key, part):
    key = jax.random.fold_in(key, 11)
    values = jnp.clip(jax.random.normal(key, (SEQS, QW, D), jnp.float32), -8.0, 8.0)
    return values.astype(jnp.bfloat16)


def draw_key_vectors(key, part):
    key = jax.random.fold_in(key, 23)
    values = jnp.clip(jax.random.normal(key, (SEQS, L, D), jnp.float32), -6.0, 6.0)
    return values.astype(jnp.bfloat16)


def set_ends(values, key, smallest, top_value):
    place = [jax.random.randint(jax.random.fold_in(key, axis), (), 0, length) for axis, length in enumerate(values.shape)]
    widest = values.shape.index(max(values.shape))
    beside = place[:widest] + [(place[widest] + 1) % values.shape[widest]] + place[widest + 1:]
    return values.at[tuple(place)].set(smallest).at[tuple(beside)].set(top_value)


def steps_of(own_key, shape, split, low, high):
    def one(dim, blocks):
        heights = jax.random.uniform(jax.random.fold_in(jax.random.fold_in(own_key, 6), dim), (blocks,), jnp.float32, low / len(split), high / len(split))
        return jnp.repeat(jnp.exp(heights), shape[dim] // blocks).reshape((-1,) + (1,) * (len(shape) - dim - 1))

    gain = one(*split[0])
    for cut in split[1:]:
        gain = gain * one(*cut)
    return gain


def bell_draw(stream_key, dims, spread, bound, cuts=(), held_as=jnp.bfloat16):
    drawn = jax.random.normal(stream_key, dims, jnp.float32) * spread
    if len(cuts) > 0:
        drawn = steps_of(stream_key, dims, cuts, -0.22, 0.18) * drawn
    return jnp.clip(drawn, min=-bound, max=bound).astype(held_as)


def setup_inputs(seed: int = 0) -> dict:
    key_of = jax.random.split(jax.random.key(seed), 9)
    queries = draw_queries(jax.random.fold_in(key_of[8], 71), 0)
    key_vectors = draw_key_vectors(jax.random.fold_in(key_of[8], 71), 0)
    value_vectors = bell_draw(key_of[2], (SEQS, L, D), 1.0, 6.0, ((0, 8), (1, 64)))
    saved_out = bell_draw(key_of[3], (SEQS, QW, D), 1.0, 6.0, ((0, 8), (1, 64)))
    grad_out = bell_draw(key_of[4], (SEQS, QW, D), 32, 192.0, ((0, 8), (1, 64)))
    out_weight = bell_draw(key_of[5], (D, D), D ** -0.5, 0.09375, ((0, 64), (1, 8)))
    window_start = set_ends(jax.random.randint(key_of[6], (SEQS,), 1, KV_DEV * N_SEQ - Q_DEV * N_SEQ + 1), jax.random.fold_in(key_of[6], 1), 1, KV_DEV * N_SEQ - Q_DEV * N_SEQ).astype(jnp.int32)
    block_order = jax.random.permutation(key_of[7], N_SEQ).astype(jnp.int32)
    return {"queries": queries, "key_vectors": key_vectors, "value_vectors": value_vectors, "saved_out": saved_out, "grad_out": grad_out, "out_weight": out_weight, "window_start": window_start, "block_order": block_order}


masked_low = -1e+30

def head_grads(query_head, key_head, value_head, context_head, row_delta, query_pos):
    length = key_head.shape[0]
    block_len = min(512, length)
    inv_root = 1.0 / math.sqrt(HD)
    key_pos = jnp.arange(length, dtype=jnp.int32)
    last_pos = jnp.max(query_pos)
    live_keys = jnp.sum((key_pos <= last_pos).astype(jnp.int32))
    loop_end = ((live_keys + block_len - 1) // block_len).astype(jnp.int32)

    def block_scores(number):
        key_block = lax.dynamic_slice_in_dim(key_head, number * block_len, block_len, 0)
        pos_block = lax.dynamic_slice_in_dim(key_pos, number * block_len, block_len, 0)
        raw = jnp.dot(query_head, key_block.T, preferred_element_type=jnp.float32) * inv_root
        seen = pos_block[None, :] <= query_pos[:, None]
        return (key_block, seen, jnp.where(seen, raw, masked_low))

    def stats_step(number, carry):
        row_max, row_sum = carry
        key_block, seen, scores = block_scores(number)
        new_max = jnp.maximum(row_max, lax.optimization_barrier(jnp.max(scores, 1)))
        row_sum = row_sum * jnp.exp(row_max - new_max) + lax.optimization_barrier(jnp.sum(jnp.where(seen, jnp.exp(scores - new_max[:, None]), 0.0), 1))
        return (new_max, row_sum)
    rows = query_head.shape[0]
    row_max, row_sum = lax.fori_loop(0, loop_end, stats_step, (jnp.full((rows,), masked_low, jnp.float32), jnp.zeros((rows,), jnp.float32)))
    log_norm = row_max + jnp.log(row_sum)

    def grad_step(number, carry):
        query_grad, key_grads, value_grads = carry
        key_block, seen, scores = block_scores(number)
        value_block = lax.dynamic_slice_in_dim(value_head, number * block_len, block_len, 0)
        attend = jnp.where(seen, jnp.exp(scores - log_norm[:, None]), 0.0)
        attend_low = attend.astype(jnp.bfloat16)
        value_piece = jnp.dot(attend_low.T, context_head, preferred_element_type=jnp.float32).astype(jnp.bfloat16)
        dprob = jnp.dot(context_head, value_block.T, preferred_element_type=jnp.float32)
        dscore = (attend * (dprob - row_delta[:, None])).astype(jnp.bfloat16)
        query_grad = query_grad + jnp.dot(dscore, key_block, preferred_element_type=jnp.float32)
        key_piece = (jnp.dot(dscore.T, query_head, preferred_element_type=jnp.float32) * inv_root).astype(jnp.bfloat16)
        key_grads = lax.dynamic_update_slice_in_dim(key_grads, key_piece, number * block_len, 0)
        value_grads = lax.dynamic_update_slice_in_dim(value_grads, value_piece, number * block_len, 0)
        return (query_grad, key_grads, value_grads)
    start_carry = (jnp.zeros((rows, HD), jnp.float32), jnp.zeros((length, HD), jnp.bfloat16), jnp.zeros((length, HD), jnp.bfloat16))
    query_grad, key_grads, value_grads = lax.fori_loop(0, loop_end, grad_step, start_carry)
    return ((query_grad * inv_root).astype(jnp.bfloat16), key_grads, value_grads)

def heads_first(array):
    return array.reshape(array.shape[0], H, HD).transpose(1, 0, 2)

def heads_back(array):
    return array.transpose(1, 0, 2).reshape(array.shape[1], H * HD)

def reference(queries, key_vectors, value_vectors, saved_out, grad_out, out_weight, window_start, block_order):
    window = queries.shape[1]
    block_rows = window // N_SEQ

    def per_sequence(total, entry):
        query_seq, key_seq, value_seq, out_seq, grad_seq, first_pos = entry
        query_pos = (first_pos + (block_order[:, None] * block_rows + jnp.arange(block_rows, dtype=jnp.int32)[None, :])).reshape(window).astype(jnp.int32)
        context = jnp.dot(grad_seq, out_weight.T, preferred_element_type=jnp.float32).astype(jnp.bfloat16)
        row_delta = lax.optimization_barrier(jnp.sum((context.astype(jnp.float32) * out_seq.astype(jnp.float32)).reshape(window, H, HD), -1))

        def one_head(parts):
            return head_grads(parts[0], parts[1], parts[2], parts[3], parts[4], query_pos)
        grads = lax.map(one_head, (heads_first(query_seq), heads_first(key_seq), heads_first(value_seq), heads_first(context), row_delta.T))
        total = total + jnp.dot(out_seq.T, grad_seq, preferred_element_type=jnp.float32)
        return (total, (heads_back(grads[0]), heads_back(grads[1]), heads_back(grads[2])))
    total, grads = lax.scan(per_sequence, jnp.zeros((D, D), jnp.float32), (queries, key_vectors, value_vectors, saved_out, grad_out, window_start))
    grad_weight = total / (queries.shape[0] * window)
    return (grads[0], grads[1], grads[2], grad_weight)
```

```python
import math

import jax
import jax.numpy as jnp
from jax import lax
from jax.experimental import pallas as pl
from jax.experimental.pallas import tpu as pltpu
from jax.sharding import PartitionSpec as P

HD = 128
NY, NZ, ND = 4, 16, 8
Q_ROWS = 8
K_ROWS = 128
WIDTH = 4096
COLS = WIDTH // NY
HEADS = COLS // HD
HALF = COLS // 2
GROUP = NY * Q_ROWS
WINDOW = NZ * GROUP
KEYS = NY * K_ROWS
W_ROWS = 64
W_COLS = WIDTH // ND
EXTRA = 128
INV_ROOT = 1.0 / math.sqrt(HD)
LOG2E = 1.0 / math.log(2.0)
LOW = -1e30
HALF_Z = NZ // 2
BF16 = jnp.bfloat16
F32 = jnp.float32
MESH = pl.DeviceIdType.MESH


def dot_nt(a, b):
    return lax.dot_general(a, b, (((1,), (1,)), ((), ())), preferred_element_type=F32)


def dot_tn(a, b):
    return lax.dot_general(a, b, (((0,), (0,)), ((), ())), preferred_element_type=F32)


def dot_nn(a, b):
    return lax.dot_general(a, b, (((1,), (0,)), ((), ())), preferred_element_type=F32)


def fold(block):
    half = block.shape[1] // 2
    return jnp.concatenate([block[:, :half], block[:, half:]], 0)


def unfold(block):
    rows = block.shape[0] // 2
    return jnp.concatenate([block[:rows], block[rows:]], 1)


def kernel(
    q_ref, so_ref, go_ref, k_ref, v_ref, w_ref, qpos_ref,
    gq_ref, gk_ref, gv_ref, gw_ref,
    kb, vb, qg, cg, wg, sog, gg,
    q_out, q_in, so_out, so_in, go_out, go_in, g_out,
    c_out, c_in, prob, row_max, row_lse, scale, delta, lse_a, lse_b,
    gks, gvs, dq, gwp,
    dq_sr, dq_sl, dq_rr, dq_rl, gw_sr, gw_sl, gw_rr, gw_rl, gq_out, gq_in,
    y_send, y_recv, d_send, d_recv, ag_send, ag_recv, l_send, l_recv, rs_send, rs_recv,
    local_sem,
):
    n = lax.axis_index("seq")
    s = lax.axis_index("dp")
    y = lax.div(n, NZ)
    z = lax.rem(n, NZ)

    def at_z(zz):
        return (y * NZ + zz, s)

    def at_y(yy):
        return (yy * NZ + z, s)

    def at_d(ss):
        return (n, ss)

    right = lax.rem(z + 1, NZ)
    left = lax.rem(z + NZ - 1, NZ)
    y_peers = [lax.rem(y + j, NY) for j in range(1, NY)]
    d_peers = [lax.rem(s + j, ND) for j in range(1, ND)]
    z_base = z - lax.rem(z, 4)
    near = [z_base + lax.rem(lax.rem(z, 4) + j, 4) for j in range(1, 4)]
    far = [lax.rem(z + 4 * j, NZ) for j in range(1, 4)]

    barrier = pltpu.get_barrier_semaphore()
    peers = (
        [at_z(right), at_z(left)]
        + [at_y(p) for p in y_peers]
        + [at_d(p) for p in d_peers]
        + [at_z(p) for p in near]
        + [at_z(p) for p in far]
    )
    for p in peers:
        pl.semaphore_signal(barrier, inc=1, device_id=p, device_id_type=MESH)

    wg[pl.ds(z, 1)] = w_ref[...][None]
    go_out[...] = fold(go_ref[...].astype(F32)).astype(BF16)
    q32 = q_ref[...].astype(F32)
    so32 = so_ref[...].astype(F32)
    for i in range(NY):
        q_out[i] = fold(q32[:, i * COLS : (i + 1) * COLS]).astype(BF16)
        so_out[i] = fold(so32[:, i * COLS : (i + 1) * COLS]).astype(BF16)
    go_in[pl.ds(y, 1)] = go_out[...][None]
    q_in[pl.ds(y, 1)] = q_out[pl.ds(y, 1)]
    so_in[pl.ds(y, 1)] = so_out[pl.ds(y, 1)]

    pl.semaphore_wait(barrier, len(peers))

    def remote(src, dst, send, recv, device):
        return pltpu.make_async_remote_copy(
            src_ref=src, dst_ref=dst, send_sem=send, recv_sem=recv,
            device_id=device, device_id_type=MESH,
        )

    def ag_right(buf, stream, k, slot):
        return remote(
            buf.at[slot], buf.at[slot], ag_send.at[stream, k], ag_recv.at[stream, slot], at_z(right)
        )

    def ag_left(buf, stream, k, slot):
        return remote(
            buf.at[slot], buf.at[slot], ag_send.at[stream, HALF_Z + k], ag_recv.at[stream, slot],
            at_z(left),
        )

    def ag_start(buf, stream):
        ag_right(buf, stream, 0, z).start()
        ag_left(buf, stream, 0, z).start()

    def ag_steps(parts):
        @pl.loop(1, HALF_Z - 1)
        def _(k):
            from_left = lax.rem(z + NZ - k, NZ)
            from_right = lax.rem(z + k, NZ)
            for buf, stream in parts:
                ag_right(buf, stream, k, from_left).wait_recv()
                ag_right(buf, stream, k, from_left).start()
                ag_left(buf, stream, k, from_right).wait_recv()
                ag_left(buf, stream, k, from_right).start()

        k = HALF_Z - 1
        for buf, stream in parts:
            slot = lax.rem(z + NZ - k, NZ)
            ag_right(buf, stream, k, slot).wait_recv()
            ag_right(buf, stream, k, slot).start()
            ag_left(buf, stream, k, lax.rem(z + k, NZ)).wait_recv()
        for buf, stream in parts:
            ag_right(buf, stream, 0, lax.rem(z + HALF_Z, NZ)).wait_recv()

    def ag_drain(buf, stream):
        @pl.loop(0, HALF_Z)
        def _(k):
            ag_right(buf, stream, k, z).wait_send()

        @pl.loop(0, HALF_Z - 1)
        def _(k):
            ag_left(buf, stream, k, z).wait_send()

    W_STREAM, Q_STREAM, C_STREAM = 0, 1, 2
    ag_start(wg, W_STREAM)

    def y_copy(kind, j, src_of, dst_of):
        p = y_peers[j]
        return remote(src_of(p), dst_of(y), y_send.at[kind, j], y_recv.at[kind, y], at_y(p))

    def y_wait(kind, dst_of, src_of):
        for j in range(NY - 1):
            p = y_peers[j]
            remote(
                src_of(p), dst_of(p), y_send.at[kind, j], y_recv.at[kind, p], at_y(p)
            ).wait_recv()

    def cols_of(p):
        return pl.ds(pl.multiple_of(p * COLS, COLS), COLS)

    kinds = [
        (lambda p: go_out, lambda p: go_in.at[p]),
        (lambda p: q_out.at[p], lambda p: q_in.at[p]),
        (lambda p: so_out.at[p], lambda p: so_in.at[p]),
        (lambda p: k_ref.at[:, cols_of(p)], lambda p: kb.at[p]),
        (lambda p: v_ref.at[:, cols_of(p)], lambda p: vb.at[p]),
        (lambda p: gvs.at[p], lambda p: gv_ref.at[:, cols_of(p)]),
        (lambda p: gks.at[p], lambda p: gk_ref.at[:, cols_of(p)]),
        (lambda p: gq_out.at[p], lambda p: gq_in.at[p]),
    ]

    def y_start(kind):
        src_of, dst_of = kinds[kind]
        for j in range(NY - 1):
            y_copy(kind, j, src_of, dst_of).start()

    def y_recv_all(kind):
        src_of, dst_of = kinds[kind]
        y_wait(kind, dst_of, src_of)

    def y_drain(kind):
        src_of, dst_of = kinds[kind]
        for j in range(NY - 1):
            y_copy(kind, j, src_of, dst_of).wait_send()

    for kind in range(5):
        y_start(kind)
    own_k = pltpu.make_async_copy(k_ref.at[:, cols_of(y)], kb.at[y], local_sem.at[0])
    own_v = pltpu.make_async_copy(v_ref.at[:, cols_of(y)], vb.at[y], local_sem.at[1])
    own_k.start()
    own_v.start()

    y_recv_all(1)
    rows = [unfold(q_in[i].astype(F32)) for i in range(NY)]
    qg[pl.ds(z, 1)] = jnp.concatenate(rows, 0).astype(BF16)[None]
    ag_start(qg, Q_STREAM)

    def d_copy(kind, j, src, dst):
        return remote(src, dst, d_send.at[kind, j], d_recv.at[kind, s], at_d(d_peers[j]))

    def d_wait(kind, buf):
        for j in range(ND - 1):
            p = d_peers[j]
            remote(
                buf.at[p], buf.at[p], d_send.at[kind, j], d_recv.at[kind, p], at_d(p)
            ).wait_recv()

    y_recv_all(0)
    for d in range(ND):
        top, off = d // (ND // 2), (d % (ND // 2)) * W_COLS
        piece = [
            go_in[i].astype(F32)[top * Q_ROWS : (top + 1) * Q_ROWS, off : off + W_COLS]
            for i in range(NY)
        ]
        g_out[d] = jnp.concatenate(piece, 0).astype(BF16)
    gg[pl.ds(s, 1)] = g_out[pl.ds(s, 1)]
    for j in range(ND - 1):
        d_copy(0, j, g_out.at[d_peers[j]], gg.at[s]).start()

    y_recv_all(2)
    rows = [unfold(so_in[i].astype(F32)) for i in range(NY)]
    sog[pl.ds(s, 1)] = jnp.concatenate(rows, 0).astype(BF16)[None]
    for j in range(ND - 1):
        d_copy(1, j, sog.at[s], sog.at[s]).start()

    ag_steps([(wg, W_STREAM), (qg, Q_STREAM)])

    d_wait(0, gg)

    @pl.loop(0, COLS // 256)
    def _(i):
        block = wg[pl.ds(4 * i, 4)].reshape(256, W_COLS)
        part = dot_nt(gg[...].reshape(ND * GROUP, W_COLS), block)
        c_out[:, :, pl.ds(pl.multiple_of(i * 256, 256), 256)] = part.reshape(
            ND, GROUP, 256
        ).astype(BF16)

    c_in[pl.ds(s, 1)] = c_out[pl.ds(s, 1)]
    for j in range(ND - 1):
        d_copy(2, j, c_out.at[d_peers[j]], c_in.at[s]).start()

    own_k.wait()
    y_recv_all(3)

    @pl.loop(0, HEADS)
    def _(h):
        lanes = pl.ds(pl.multiple_of(h * HD, HD), HD)
        query = qg[:, :, lanes].reshape(WINDOW, HD)
        key_iota = lax.broadcasted_iota(jnp.int32, (K_ROWS, WINDOW), 0)
        scores = []
        for b in range(NY):
            raw = dot_nt(kb[b, :, lanes], query) * (INV_ROOT * LOG2E)
            seen = key_iota <= qpos_ref[...] - (b * NZ + z) * K_ROWS
            scores.append(jnp.where(seen, raw, LOW))
        top = jnp.max(scores[0], 0, keepdims=True)
        for b in range(1, NY):
            top = jnp.maximum(top, jnp.max(scores[b], 0, keepdims=True))
        total = jnp.zeros((1, WINDOW), F32)
        for b in range(NY):
            e = jnp.exp2(scores[b] - top)
            total = total + jnp.sum(e, 0, keepdims=True)
            prob[h, pl.ds(b * K_ROWS, K_ROWS)] = e.astype(BF16)
        row_max[pl.ds(h, 1), :] = top
        row_lse[pl.ds(h, 1), :] = top + jnp.log2(total)

    def lse_copy(level, j, src, dst, zz):
        return remote(src, dst, l_send.at[level, j], l_recv.at[level, j], at_z(zz))

    for j in range(3):
        lse_copy(0, j, row_lse, lse_a.at[j], near[j]).start()

    d_wait(2, c_in)
    context = c_in[0].astype(F32)
    for d in range(1, ND):
        context = context + c_in[d].astype(F32)
    context = context.astype(BF16)
    product = context.astype(F32) * sog[pl.ds(s, 1)].reshape(GROUP, COLS).astype(F32)
    lane = lax.broadcasted_iota(jnp.int32, (GROUP, EXTRA), 1)
    sums = jnp.zeros((GROUP, EXTRA), F32)
    for h in range(HEADS):
        one = jnp.sum(product[:, h * HD : (h + 1) * HD], 1, keepdims=True)
        sums = jnp.where(lax.rem(lane, HEADS) == h, one, sums)
    high = sums.astype(BF16).astype(F32)
    rest = jnp.where(lane < HEADS, high, sums - high)
    cg[pl.ds(z, 1)] = jnp.concatenate([context.astype(F32), rest], 1).astype(BF16)[None]
    ag_start(cg, C_STREAM)

    def joined(first, others):
        most = first
        for o in others:
            most = jnp.maximum(most, o)
        total = jnp.exp2(first - most)
        for o in others:
            total = total + jnp.exp2(o - most)
        return most + jnp.log2(total)

    for j in range(3):
        lse_copy(0, j, row_lse, lse_a.at[j], near[j]).wait()
    row_lse[...] = joined(row_lse[...], [lse_a[j] for j in range(3)])
    for j in range(3):
        lse_copy(1, j, row_lse, lse_b.at[j], far[j]).start()

    d_wait(1, sog)

    @pl.loop(0, COLS // 256)
    def _(i):
        block = sog[:, :, pl.ds(pl.multiple_of(i * 256, 256), 256)].reshape(ND * GROUP, 256)
        part = dot_tn(block, gg[...].reshape(ND * GROUP, W_COLS))
        gwp[pl.ds(4 * i, 4)] = part.reshape(4, W_ROWS, W_COLS)

    for j in range(3):
        lse_copy(1, j, row_lse, lse_b.at[j], far[j]).wait()
    scale[...] = jnp.exp2(row_max[...] - joined(row_lse[...], [lse_b[j] for j in range(3)]))

    ag_steps([(cg, C_STREAM)])
    own_v.wait()
    y_recv_all(4)

    pick_row = lax.broadcasted_iota(jnp.int32, (HEADS, EXTRA), 0)
    pick_lane = lax.broadcasted_iota(jnp.int32, (HEADS, EXTRA), 1)
    pick = jnp.where(
        (lax.rem(pick_lane, HEADS) == pick_row) & (pick_lane < 2 * HEADS), 1.0, 0.0
    ).astype(BF16)
    delta[...] = dot_nt(pick, cg[:, :, COLS:].reshape(WINDOW, EXTRA))

    @pl.loop(0, HEADS)
    def _(h):
        lanes = pl.ds(pl.multiple_of(h * HD, HD), HD)
        query = qg[:, :, lanes].reshape(WINDOW, HD)
        ctx = cg[:, :, lanes].reshape(WINDOW, HD)
        row_scale = scale[pl.ds(h, 1), :]
        row_delta = delta[pl.ds(h, 1), :]
        total = jnp.zeros((WINDOW, HD), F32)
        for b in range(NY):
            attend = prob[h, pl.ds(b * K_ROWS, K_ROWS)].astype(F32) * row_scale
            gvs[b, :, lanes] = dot_nn(attend.astype(BF16), ctx).astype(BF16)
            dprob = dot_nt(vb[b, :, lanes], ctx)
            dscore = (attend * (dprob - row_delta)).astype(BF16)
            gks[b, :, lanes] = (dot_nn(dscore, query) * INV_ROOT).astype(BF16)
            total = total + dot_tn(dscore, kb[b, :, lanes])
        dq[:, :, lanes] = total.reshape(NZ, GROUP, HD)

    y_start(5)
    y_start(6)
    own_gv = pltpu.make_async_copy(gvs.at[y], gv_ref.at[:, cols_of(y)], local_sem.at[2])
    own_gk = pltpu.make_async_copy(gks.at[y], gk_ref.at[:, cols_of(y)], local_sem.at[3])
    own_gv.start()
    own_gk.start()

    parts = [
        (dq, dq_sr, dq_sl, dq_rr, dq_rl, 0),
        (gwp, gw_sr, gw_sl, gw_rr, gw_rl, 1),
    ]

    def rs_right(part, k):
        _, sr, _, rr, _, stream = part
        return remote(
            sr.at[k], rr.at[k], rs_send.at[stream, k], rs_recv.at[stream, k], at_z(right)
        )

    def rs_left(part, k):
        _, _, sl, _, rl, stream = part
        return remote(
            sl.at[k], rl.at[k], rs_send.at[stream, HALF_Z + k], rs_recv.at[stream, HALF_Z + k],
            at_z(left),
        )

    for part in parts:
        own, sr, sl = part[:3]
        sr[0] = own[pl.ds(lax.rem(z + HALF_Z, NZ), 1)][0].astype(BF16)
        rs_right(part, 0).start()
        sl[0] = own[pl.ds(lax.rem(z + NZ - (HALF_Z - 1), NZ), 1)][0].astype(BF16)
        rs_left(part, 0).start()

    @pl.loop(1, HALF_Z - 1)
    def _(k):
        for part in parts:
            own, sr, sl, rr, rl, _ = part
            rs_right(part, k - 1).wait_recv()
            mine = own[pl.ds(lax.rem(z + HALF_Z - k, NZ), 1)]
            sr[pl.ds(k, 1)] = (rr[pl.ds(k - 1, 1)].astype(F32) + mine).astype(BF16)
            rs_right(part, k).start()
            rs_left(part, k - 1).wait_recv()
            mine = own[pl.ds(lax.rem(z + NZ - (HALF_Z - 1) + k, NZ), 1)]
            sl[pl.ds(k, 1)] = (rl[pl.ds(k - 1, 1)].astype(F32) + mine).astype(BF16)
            rs_left(part, k).start()

    k = HALF_Z - 1
    for part in parts:
        own, sr, sl, rr, rl, _ = part
        rs_right(part, k - 1).wait_recv()
        mine = own[pl.ds(lax.rem(z + HALF_Z - k, NZ), 1)][0]
        sr[k] = (rr[k - 1].astype(F32) + mine).astype(BF16)
        rs_right(part, k).start()

    def rs_result(part):
        own, _, _, rr, rl, _ = part
        rs_left(part, HALF_Z - 2).wait_recv()
        rs_right(part, HALF_Z - 1).wait_recv()
        return (
            own[pl.ds(z, 1)][0] + rr[HALF_Z - 1].astype(F32) + rl[HALF_Z - 2].astype(F32)
        )

    query_grad = rs_result(parts[0]) * INV_ROOT
    for i in range(NY):
        gq_out[i] = fold(query_grad[i * Q_ROWS : (i + 1) * Q_ROWS]).astype(BF16)
    gq_in[pl.ds(y, 1)] = gq_out[pl.ds(y, 1)]
    y_start(7)
    gw_ref[...] = rs_result(parts[1]) * (1.0 / (ND * WINDOW))
    y_recv_all(7)
    for i in range(NY):
        gq_ref[:, i * COLS : (i + 1) * COLS] = unfold(gq_in[i].astype(F32)).astype(BF16)

    for buf, stream in ((wg, W_STREAM), (qg, Q_STREAM), (cg, C_STREAM)):
        ag_drain(buf, stream)
    for j in range(ND - 1):
        d_copy(0, j, g_out.at[d_peers[j]], gg.at[s]).wait_send()
        d_copy(1, j, sog.at[s], sog.at[s]).wait_send()
        d_copy(2, j, c_out.at[d_peers[j]], c_in.at[s]).wait_send()
    for part in parts:

        @pl.loop(0, HALF_Z)
        def _(k):
            rs_right(part, k).wait_send()

        @pl.loop(0, HALF_Z - 1)
        def _(k):
            rs_left(part, k).wait_send()

    y_recv_all(5)
    y_recv_all(6)
    own_gv.wait()
    own_gk.wait()
    for kind in range(8):
        y_drain(kind)


def on_device(
    queries, key_vectors, value_vectors, saved_out, grad_out, out_weight, window_start, block_order
):
    blocks = block_order.reshape(NY, NZ).T.reshape(NZ * NY, 1) * Q_ROWS
    query_pos = window_start[0] + blocks + jnp.arange(Q_ROWS, dtype=jnp.int32)[None, :]
    vmem = pl.BlockSpec(memory_space=pltpu.VMEM)
    hbm = pl.BlockSpec(memory_space=pl.ANY)

    def buf(*shape, dtype=BF16):
        return pltpu.VMEM(shape, dtype)

    dma = pltpu.SemaphoreType.DMA
    scratch = [
        buf(NY, K_ROWS, COLS), buf(NY, K_ROWS, COLS),
        buf(NZ, GROUP, COLS), buf(NZ, GROUP, COLS + EXTRA), buf(NZ, W_ROWS, W_COLS),
        buf(ND, GROUP, COLS), buf(ND, GROUP, W_COLS),
        buf(NY, 2 * Q_ROWS, HALF), buf(NY, 2 * Q_ROWS, HALF),
        buf(NY, 2 * Q_ROWS, HALF), buf(NY, 2 * Q_ROWS, HALF),
        buf(2 * Q_ROWS, WIDTH // 2), buf(NY, 2 * Q_ROWS, WIDTH // 2),
        buf(ND, GROUP, W_COLS),
        buf(ND, GROUP, COLS), buf(ND, GROUP, COLS),
        buf(HEADS, KEYS, WINDOW),
        buf(HEADS, WINDOW, dtype=F32), buf(HEADS, WINDOW, dtype=F32),
        buf(HEADS, WINDOW, dtype=F32), buf(HEADS, WINDOW, dtype=F32),
        buf(3, HEADS, WINDOW, dtype=F32), buf(3, HEADS, WINDOW, dtype=F32),
        buf(NY, K_ROWS, COLS), buf(NY, K_ROWS, COLS),
        buf(NZ, GROUP, COLS, dtype=F32), buf(NZ, W_ROWS, W_COLS, dtype=F32),
        buf(HALF_Z, GROUP, COLS), buf(HALF_Z, GROUP, COLS),
        buf(HALF_Z, GROUP, COLS), buf(HALF_Z, GROUP, COLS),
        buf(HALF_Z, W_ROWS, W_COLS), buf(HALF_Z, W_ROWS, W_COLS),
        buf(HALF_Z, W_ROWS, W_COLS), buf(HALF_Z, W_ROWS, W_COLS),
        buf(NY, 2 * Q_ROWS, HALF), buf(NY, 2 * Q_ROWS, HALF),
        dma((8, NY - 1)), dma((8, NY)),
        dma((3, ND - 1)), dma((3, ND)),
        dma((3, NZ)), dma((3, NZ)),
        dma((2, 3)), dma((2, 3)),
        dma((2, NZ)), dma((2, NZ)),
        dma((4,)),
    ]
    outs = pl.pallas_call(
        kernel,
        out_shape=(
            jax.ShapeDtypeStruct((Q_ROWS, WIDTH), BF16),
            jax.ShapeDtypeStruct((K_ROWS, WIDTH), BF16),
            jax.ShapeDtypeStruct((K_ROWS, WIDTH), BF16),
            jax.ShapeDtypeStruct((W_ROWS, W_COLS), F32),
        ),
        in_specs=[vmem, vmem, vmem, hbm, hbm, vmem, vmem],
        out_specs=(vmem, hbm, hbm, vmem),
        scratch_shapes=scratch,
        compiler_params=pltpu.CompilerParams(
            collective_id=0, has_side_effects=True, vmem_limit_bytes=48 * 1024 * 1024
        ),
        name="attention_backward",
    )(
        queries[0], saved_out[0], grad_out[0], key_vectors[0], value_vectors[0], out_weight,
        query_pos.reshape(1, WINDOW),
    )
    return (outs[0][None], outs[1][None], outs[2][None], outs[3])


def solution(mesh):
    rows = P("dp", "seq", None)
    return jax.shard_map(
        on_device,
        mesh=mesh,
        in_specs=(rows, rows, rows, rows, rows, P("seq", "dp"), P("dp"), P()),
        out_specs=(rows, rows, rows, P("seq", "dp")),
        check_vma=False,
    )
```

```python
import math

import jax
import jax.numpy as jnp
from jax import lax
from jax.experimental import pallas as pl
from jax.experimental.pallas import tpu as pltpu
from jax.sharding import PartitionSpec as P

HD = 128
NY, NZ, ND = 4, 16, 8
Q_ROWS = 8
K_ROWS = 128
WIDTH = 4096
COLS = WIDTH // NY
HEADS = COLS // HD
HALF = COLS // 2
GROUP = NY * Q_ROWS
WINDOW = NZ * GROUP
KEYS = NY * K_ROWS
W_ROWS = 64
W_COLS = WIDTH // ND
INV_ROOT = 1.0 / math.sqrt(HD)
LOG2E = 1.0 / math.log(2.0)
LOW = -1e30
HALF_Z = NZ // 2
CHUNKS = 4
CHUNK = COLS // CHUNKS
BLOCK = WINDOW // CHUNKS
SLOT = HEADS * GROUP + 2 * HEADS
NEAR = 4
JUMP = 5
VMEM_BYTES = 64 * 1024 * 1024
BF16 = jnp.bfloat16
F32 = jnp.float32
MESH = pl.DeviceIdType.MESH


def dot_nt(a, b):
    return lax.dot_general(a, b, (((1,), (1,)), ((), ())), preferred_element_type=F32)


def dot_tn(a, b):
    return lax.dot_general(a, b, (((0,), (0,)), ((), ())), preferred_element_type=F32)


def dot_nn(a, b):
    return lax.dot_general(a, b, (((1,), (0,)), ((), ())), preferred_element_type=F32)


def fold(block):
    half = block.shape[1] // 2
    return jnp.concatenate([block[:, :half], block[:, half:]], 0)


def unfold(block):
    rows = block.shape[0] // 2
    return jnp.concatenate([block[:rows], block[rows:]], 1)


def kernel(
    q_ref, so_ref, go_ref, k_ref, v_ref, w_ref, order_ref, start_ref,
    gq_ref, gk_ref, gv_ref, gw_ref,
    q_own, so_own, go_own,
    kb, vb, qg, cg, wg, sog, gg,
    q_out, q_in, so_out, so_in, go_out, go_in, g_out,
    c_out, c_in, prob, query_pos, row_max, lse_own, lse_near, lse_a, lse_b, scale, delta,
    gvs, gks, dq, gwp, gw_out,
    dq_send, dq_recv, gw_sr, gw_sl, gw_rr, gw_rl, gq_out, gq_in, gq_all,
    y_send, y_recv, d_send, d_recv, ag_send, ag_recv, l_send, l_recv,
    dq_ssem, dq_rsem, gw_ssem, gw_rsem, local_sem,
):
    n = lax.axis_index("seq")
    s = lax.axis_index("dp")
    y = lax.div(n, NZ)
    z = lax.rem(n, NZ)

    def at_y(yy):
        return (yy * NZ + z, s)

    def at_d(ss):
        return (n, ss)

    def z_off(j):
        return lax.rem(z + (j + NZ), NZ)

    def at_z(j):
        return (y * NZ + z_off(j), s)

    y_peers = [lax.rem(y + j, NY) for j in range(1, NY)]
    d_peers = [lax.rem(s + j, ND) for j in range(1, ND)]
    z_low = lax.rem(z, 4)
    z_high = lax.div(z, 4)

    def nth_block(i):
        turn = i + lax.div(i, 2) - 2 * lax.div(i, 3)
        toward = 2 * lax.div(z_low, 2) - 1
        return lax.rem(z_high + 8 + toward * turn, CHUNKS)

    near = [(y * NZ + z - z_low + lax.rem(z_low + j, 4), s) for j in range(1, 4)]
    far = [at_z(4 * j) for j in range(1, 4)]

    barrier = pltpu.get_barrier_semaphore()
    peers = (
        [at_z(1), at_z(-1), at_z(JUMP), at_z(-JUMP)]
        + [at_y(p) for p in y_peers]
        + [at_d(p) for p in d_peers]
        + near
        + far
    )
    for p in peers:
        pl.semaphore_signal(barrier, inc=1, device_id=p, device_id_type=MESH)

    def cols_of(p):
        return pl.ds(pl.multiple_of(p * COLS, COLS), COLS)

    loads = [
        pltpu.make_async_copy(src, dst, local_sem.at[i])
        for i, (src, dst) in enumerate([
            (go_ref, go_own),
            (q_ref, q_own),
            (so_ref, so_own),
            (w_ref, wg.at[z]),
            (k_ref.at[:, cols_of(y)], kb.at[y]),
            (v_ref.at[:, cols_of(y)], vb.at[y]),
        ])
    ]
    for load in loads:
        load.start()

    row = lax.broadcasted_iota(jnp.int32, (NY * NZ, WINDOW), 0)
    place = lax.broadcasted_iota(jnp.int32, (NY * NZ, WINDOW), 1)
    holder = ((place >> 3) & (NY - 1)) * NZ + (place >> 5)
    select = jnp.where(row == holder, 1.0, 0.0).astype(BF16)
    order = jnp.broadcast_to(order_ref[...].astype(F32), (8, NY * NZ)).astype(BF16)
    inside = (lax.broadcasted_iota(jnp.int32, (8, WINDOW), 1) & (Q_ROWS - 1)).astype(F32)
    query_pos[...] = dot_nn(order, select) * Q_ROWS + inside + start_ref[0].astype(F32)

    loads[0].wait()
    go_out[...] = fold(go_own[...].astype(F32)).astype(BF16)
    loads[1].wait()
    loads[2].wait()
    q32 = q_own[...].astype(F32)
    so32 = so_own[...].astype(F32)
    for i in range(NY):
        q_out[i] = fold(q32[:, i * COLS : (i + 1) * COLS]).astype(BF16)
        so_out[i] = fold(so32[:, i * COLS : (i + 1) * COLS]).astype(BF16)
    go_in[pl.ds(y, 1)] = go_out[...][None]
    q_in[pl.ds(y, 1)] = q_out[pl.ds(y, 1)]
    so_in[pl.ds(y, 1)] = so_out[pl.ds(y, 1)]
    loads[3].wait()

    pl.semaphore_wait(barrier, len(peers))

    def remote(src, dst, send, recv, device):
        return pltpu.make_async_remote_copy(
            src_ref=src, dst_ref=dst, send_sem=send, recv_sem=recv,
            device_id=device, device_id_type=MESH,
        )

    streams = [wg, qg, cg]

    def z_send(stream, sem, distance, hop):
        buf, slot = streams[stream], z_off(-distance)
        return remote(
            buf.at[slot], buf.at[slot], ag_send.at[stream, sem], ag_recv.at[stream, slot], at_z(hop)
        )

    def z_arrived(stream, distance):
        z_send(stream, 0, distance, 1).wait_recv()

    z_sends = {}

    def z_go(stream, distance, hop):
        sem = z_sends.get(stream, 0)
        z_sends[stream] = sem + 1
        z_send(stream, sem, distance, hop).start()

    def ring_start(stream):
        z_go(stream, 0, 1)
        z_go(stream, 0, -1)

    def ring_step(stream, k):
        z_arrived(stream, k)
        if k < HALF_Z:
            z_go(stream, k, 1)
            z_arrived(stream, -k)
            if k < HALF_Z - 1:
                z_go(stream, -k, -1)

    def wave_start(stream):
        z_go(stream, 0, 1)
        z_go(stream, 0, -1)
        z_go(stream, 0, JUMP)
        z_go(stream, 0, -JUMP)

    def wave_near(stream, k):
        for sign in (1, -1):
            z_arrived(stream, sign * k)
            if k < NEAR:
                z_go(stream, sign * k, sign)

    def wave_far(stream, k):
        for sign, last in ((1, HALF_Z), (-1, HALF_Z - 1)):
            distance = NEAR + k
            if distance <= last:
                z_arrived(stream, sign * distance)
            if distance < last:
                z_go(stream, sign * distance, sign)

    def z_drain(stream):
        @pl.loop(0, z_sends[stream])
        def _(sem):
            z_send(stream, sem, 0, 1).wait_send()

    W, Q, C = 0, 1, 2

    kinds = [
        (lambda p: go_out, lambda p: go_in.at[p]),
        (lambda p: q_out.at[p], lambda p: q_in.at[p]),
        (lambda p: so_out.at[p], lambda p: so_in.at[p]),
        (lambda p: k_ref.at[:, cols_of(p)], lambda p: kb.at[p]),
        (lambda p: v_ref.at[:, cols_of(p)], lambda p: vb.at[p]),
        (lambda p: gvs.at[p], lambda p: gv_ref.at[:, cols_of(p)]),
        (lambda p: gks.at[p], lambda p: gk_ref.at[:, cols_of(p)]),
        (lambda p: gq_out.at[p], lambda p: gq_in.at[p]),
    ]
    GV, GK, GQ = 5, 6, 7

    def y_copy(kind, j, slot):
        src_of, dst_of = kinds[kind]
        p = y_peers[j]
        return remote(
            src_of(p), dst_of(slot), y_send.at[kind, j], y_recv.at[kind, slot], at_y(p)
        )

    def y_start(kind):
        for j in range(NY - 1):
            y_copy(kind, j, y).start()

    def y_arrived(kind):
        for j in range(NY - 1):
            y_copy(kind, j, y_peers[j]).wait_recv()

    def y_drain(kind):
        for j in range(NY - 1):
            y_copy(kind, j, y).wait_send()

    d_sends = []

    def d_start(kind, src_of, buf):
        for j in range(ND - 1):
            p = d_peers[j]
            copy = remote(
                src_of(p), buf.at[s], d_send.at[kind, j], d_recv.at[kind, s], at_d(p)
            )
            copy.start()
            d_sends.append(copy)

    def d_arrived(kind, buf):
        for j in range(ND - 1):
            p = d_peers[j]
            remote(
                buf.at[p], buf.at[p], d_send.at[kind, j], d_recv.at[kind, p], at_d(p)
            ).wait_recv()

    def partial_context(i):
        block = wg[pl.ds(4 * nth_block(i), 4)].reshape(CHUNK, W_COLS)
        part = dot_nt(gg[...].reshape(ND * GROUP, W_COLS), block)
        c_out[i] = part.reshape(ND, GROUP, CHUNK).astype(BF16)
        c_in[i, pl.ds(s, 1)] = c_out[i, pl.ds(s, 1)]
        d_start(2 + i, lambda p: c_out.at[i, p], c_in.at[i])

    def gw_right(k):
        return remote(gw_sr.at[k], gw_rr.at[k], gw_ssem.at[k], gw_rsem.at[k], at_z(1))

    def gw_left(k):
        i = HALF_Z + k
        return remote(gw_sl.at[k], gw_rl.at[k], gw_ssem.at[i], gw_rsem.at[i], at_z(-1))

    def gw_step(k):
        mine = gwp[pl.ds(z_off(HALF_Z - k), 1)][0]
        if k > 0:
            gw_right(k - 1).wait_recv()
            mine = mine + gw_rr[k - 1].astype(F32)
        gw_sr[k] = mine.astype(BF16)
        gw_right(k).start()
        if k < HALF_Z - 1:
            mine = gwp[pl.ds(z_off(k + 1 - HALF_Z), 1)][0]
            if k > 0:
                gw_left(k - 1).wait_recv()
                mine = mine + gw_rl[k - 1].astype(F32)
            gw_sl[k] = mine.astype(BF16)
            gw_left(k).start()

    gw_store = pltpu.make_async_copy(gw_out, gw_ref, local_sem.at[6])

    def gw_end():
        gw_left(HALF_Z - 2).wait_recv()
        gw_right(HALF_Z - 1).wait_recv()
        total = (
            gwp[pl.ds(z, 1)][0]
            + gw_rr[HALF_Z - 1].astype(F32)
            + gw_rl[HALF_Z - 2].astype(F32)
        )
        gw_out[...] = total * (1.0 / (ND * WINDOW))
        gw_store.start()

    def softmax_head(h):
        lanes = pl.ds(pl.multiple_of(h * HD, HD), HD)
        query = qg[:, :, lanes].reshape(WINDOW, HD)
        key_place = lax.broadcasted_iota(jnp.int32, (K_ROWS, WINDOW), 0).astype(F32)
        scores = []
        for b in range(NY):
            raw = dot_nt(kb[b, :, lanes], query) * (INV_ROOT * LOG2E)
            first_key = ((b * NZ + z) * K_ROWS).astype(F32)
            seen = key_place <= query_pos[0:1, :] - first_key
            scores.append(jnp.where(seen, raw, LOW))
        top = jnp.max(scores[0], 0, keepdims=True)
        for b in range(1, NY):
            top = jnp.maximum(top, jnp.max(scores[b], 0, keepdims=True))
        total = jnp.zeros((1, WINDOW), F32)
        for b in range(NY):
            e = jnp.exp2(scores[b] - top)
            total = total + jnp.sum(e, 0, keepdims=True)
            prob[h, b * K_ROWS : (b + 1) * K_ROWS] = e.astype(BF16)
        row_max[pl.ds(h, 1), :] = top
        lse_own[pl.ds(h, 1), :] = top + jnp.log2(total)

    def lse_copy(level, j):
        src, dst = ((lse_own, lse_a), (lse_near, lse_b))[level]
        i = level * 3 + j
        return remote(src, dst.at[j], l_send.at[i], l_recv.at[i], (near, far)[level][j])

    def joined(first, others):
        most = first
        for o in others:
            most = jnp.maximum(most, o)
        total = jnp.exp2(first - most)
        for o in others:
            total = total + jnp.exp2(o - most)
        return most + jnp.log2(total)

    def lse_start():
        for j in range(3):
            lse_copy(0, j).start()

    def lse_next():
        for j in range(3):
            lse_copy(0, j).wait()
        lse_near[...] = joined(lse_own[...], [lse_a[j] for j in range(3)])
        for j in range(3):
            lse_copy(1, j).start()

    def lse_end():
        for j in range(3):
            lse_copy(1, j).wait()
        lse = joined(lse_near[...], [lse_b[j] for j in range(3)])
        scale[...] = jnp.exp2(row_max[...] - lse)

    def both(k):
        ring_step(W, k)
        ring_step(Q, k)

    y_start(1)
    y_start(0)
    ring_start(W)
    for kind in range(2, 5):
        y_start(kind)

    y_arrived(1)
    rows = [unfold(q_in[i].astype(F32)) for i in range(NY)]
    qg[pl.ds(z, 1)] = jnp.concatenate(rows, 0).astype(BF16)[None]
    ring_start(Q)

    y_arrived(0)
    for d in range(ND):
        top, off = d // (ND // 2), (d % (ND // 2)) * W_COLS
        piece = [
            go_in[i].astype(F32)[top * Q_ROWS : (top + 1) * Q_ROWS, off : off + W_COLS]
            for i in range(NY)
        ]
        g_out[d] = jnp.concatenate(piece, 0).astype(BF16)
    gg[pl.ds(s, 1)] = g_out[pl.ds(s, 1)]
    d_start(0, lambda p: g_out.at[p], gg)

    both(1)
    y_arrived(2)
    rows = [unfold(so_in[i].astype(F32)) for i in range(NY)]
    sog[pl.ds(s, 1)] = jnp.concatenate(rows, 0).astype(BF16)[None]
    d_start(1, lambda p: sog.at[s], sog)

    both(2)
    both(3)
    d_arrived(0, gg)
    partial_context(0)
    both(4)
    both(5)
    partial_context(1)
    both(6)
    d_arrived(1, sog)
    for i in range(CHUNKS):
        block = sog[:, :, i * CHUNK : (i + 1) * CHUNK].reshape(ND * GROUP, CHUNK)
        piece = dot_tn(block, gg[...].reshape(ND * GROUP, W_COLS))
        gwp[4 * i : 4 * i + 4] = piece.reshape(4, W_ROWS, W_COLS)
    both(7)
    partial_context(2)
    ring_step(W, 8)
    partial_context(3)
    ring_step(Q, 8)

    loads[4].wait()
    y_arrived(3)

    @pl.loop(0, HEADS, unroll=2)
    def _(h):
        softmax_head(h)

    lse_start()

    lane = lax.broadcasted_iota(jnp.int32, (GROUP, HD), 1)
    sums = jnp.zeros((GROUP, HD), F32)
    for i in range(CHUNKS):
        d_arrived(2 + i, c_in.at[i])
        context = c_in[i, 0].astype(F32)
        for d in range(1, ND):
            context = context + c_in[i, d].astype(F32)
        context = context.astype(BF16)
        chunk = nth_block(i)
        lanes = pl.ds(pl.multiple_of(chunk * CHUNK, CHUNK), CHUNK)
        product = context.astype(F32) * sog[pl.ds(s, 1), :, lanes][0].astype(F32)
        for j in range(CHUNK // HD):
            h = chunk * (CHUNK // HD) + j
            own = slice(j * HD, (j + 1) * HD)
            cg[pl.ds(z, 1), pl.ds(pl.multiple_of(h * GROUP, GROUP), GROUP), :] = context[:, own][None]
            one = jnp.sum(product[:, own], 1, keepdims=True)
            sums = jnp.where((lane & (HEADS - 1)) == h, one, sums)
    high = sums.astype(BF16).astype(F32)
    rest = jnp.where(lane < HEADS, high, sums - high).astype(BF16)
    row = lax.broadcasted_iota(jnp.int32, (GROUP, HD), 0)
    place = jnp.where(lane == row + z_low * GROUP, 1.0, 0.0).astype(BF16)
    cg[pl.ds(z, 1), HEADS * GROUP :, :] = dot_tn(rest, place)[: 2 * HEADS].astype(BF16)[None]
    wave_start(C)
    wave_near(C, 1)
    lse_next()
    wave_near(C, 2)
    gw_step(0)
    wave_far(C, 1)
    wave_near(C, 3)
    gw_step(1)
    wave_far(C, 2)
    lse_end()
    wave_near(C, 4)
    gw_step(2)
    wave_far(C, 3)
    gw_step(3)
    wave_far(C, 4)
    loads[5].wait()
    y_arrived(4)

    chains = [(1, HALF_Z, 4), (-1, HALF_Z - 1, 3), (1, NEAR, 4), (-1, NEAR, 4)]

    def dq_copy(c, k):
        sign, reach, length = chains[c]
        hop = sign * JUMP if reach > NEAR and k == length - 1 else sign
        i = 4 * c + k
        return remote(dq_send.at[i], dq_recv.at[i], dq_ssem.at[i], dq_rsem.at[i], at_z(hop))

    def dq_step(k):
        for c, (sign, reach, length) in enumerate(chains):
            if k < length:
                mine = dq[pl.ds(z_off(sign * (reach - k)), 1)][0]
                if k > 0:
                    dq_copy(c, k - 1).wait_recv()
                    mine = mine + dq_recv[4 * c + k - 1].astype(F32)
                dq_send[4 * c + k] = mine.astype(BF16)
                dq_copy(c, k).start()

    def dq_end():
        total = dq[pl.ds(z, 1)][0]
        for c in (2, 3, 0, 1):
            last = chains[c][2] - 1
            dq_copy(c, last).wait_recv()
            total = total + dq_recv[4 * c + last].astype(F32)
        total = total * INV_ROOT
        for i in range(NY):
            gq_out[i] = fold(total[i * Q_ROWS : (i + 1) * Q_ROWS]).astype(BF16)
        gq_in[pl.ds(y, 1)] = gq_out[pl.ds(y, 1)]
        y_start(GQ)

    for i in range(CHUNKS):
        tile = cg[4 * i : 4 * i + 4, HEADS * GROUP :, :].astype(F32)
        tile = tile[0] + tile[1] + tile[2] + tile[3]
        delta[:, i * BLOCK : (i + 1) * BLOCK] = tile[:HEADS] + tile[HEADS:]

    @pl.loop(0, HEADS, unroll=2)
    def _(h):
        lanes = pl.ds(pl.multiple_of(h * HD, HD), HD)
        query = qg[:, :, lanes].reshape(WINDOW, HD)
        head_rows = pl.ds(pl.multiple_of(h * GROUP, GROUP), GROUP)
        ctx = cg[:, head_rows, :].reshape(WINDOW, HD)
        attend = prob[h].astype(F32) * scale[pl.ds(h, 1), :]
        value_grad = dot_nn(attend.astype(BF16), ctx)
        dprob = dot_nt(vb[:, :, lanes].reshape(KEYS, HD), ctx)
        dscore = (attend * (dprob - delta[pl.ds(h, 1), :])).astype(BF16)
        key_grad = dot_nn(dscore, query) * INV_ROOT
        query_grad = dot_tn(dscore, kb[:, :, lanes].reshape(KEYS, HD))
        gvs[:, :, lanes] = value_grad.astype(BF16).reshape(NY, K_ROWS, HD)
        gks[:, :, lanes] = key_grad.astype(BF16).reshape(NY, K_ROWS, HD)
        dq[:, :, lanes] = query_grad.reshape(NZ, GROUP, HD)

    dq_step(0)
    y_start(GV)
    y_start(GK)
    own_stores = [
        pltpu.make_async_copy(src.at[y], dst.at[:, cols_of(y)], local_sem.at[7 + i])
        for i, (src, dst) in enumerate([(gvs, gv_ref), (gks, gk_ref)])
    ]
    for store in own_stores:
        store.start()
    dq_step(1)
    gw_step(4)
    z_drain(W)
    z_drain(Q)
    dq_step(2)
    gw_step(5)
    z_drain(C)
    dq_step(3)
    gw_step(6)
    for copy in d_sends:
        copy.wait_send()
    for kind in range(5):
        y_drain(kind)
    gw_step(7)
    dq_end()
    gw_end()
    for k in range(HALF_Z):
        gw_right(k).wait_send()
    for k in range(HALF_Z - 1):
        gw_left(k).wait_send()
    for c, (_, _, length) in enumerate(chains):
        for k in range(length):
            dq_copy(c, k).wait_send()
    y_arrived(GQ)
    for i in range(NY):
        gq_all[:, i * COLS : (i + 1) * COLS] = unfold(gq_in[i].astype(F32)).astype(BF16)
    gq_store = pltpu.make_async_copy(gq_all, gq_ref, local_sem.at[9])
    gq_store.start()
    for kind in (GV, GK):
        y_arrived(kind)
    for kind in (GV, GK, GQ):
        y_drain(kind)
    for store in own_stores:
        store.wait()
    gw_store.wait()
    gq_store.wait()


def deliver(*refs):
    count = (len(refs) - 1) // 3
    sources, results, stages = (refs[i * count : (i + 1) * count] for i in range(3))
    sem = refs[-1]
    fetches = [
        pltpu.make_async_copy(sources[i], stages[i], sem.at[0, i]) for i in range(count)
    ]
    stores = [
        pltpu.make_async_copy(stages[i], results[i], sem.at[1, i]) for i in range(count)
    ]
    for fetch in fetches:
        fetch.start()
    for fetch, store in zip(fetches, stores):
        fetch.wait()
        store.start()
    for store in stores:
        store.wait()


def on_device(
    queries, key_vectors, value_vectors, saved_out, grad_out, out_weight, window_start, block_order
):
    vmem = pl.BlockSpec(memory_space=pltpu.VMEM)
    smem = pl.BlockSpec(memory_space=pltpu.SMEM)
    hbm = pl.BlockSpec(memory_space=pl.ANY)

    def buf(*shape, dtype=BF16):
        return pltpu.VMEM(shape, dtype)

    dma = pltpu.SemaphoreType.DMA
    rows = (HEADS, WINDOW)
    scratch = [
        buf(Q_ROWS, WIDTH), buf(Q_ROWS, WIDTH), buf(Q_ROWS, WIDTH),
        buf(NY, K_ROWS, COLS), buf(NY, K_ROWS, COLS),
        buf(NZ, GROUP, COLS), buf(NZ, SLOT, HD), buf(NZ, W_ROWS, W_COLS),
        buf(ND, GROUP, COLS), buf(ND, GROUP, W_COLS),
        buf(NY, 2 * Q_ROWS, HALF), buf(NY, 2 * Q_ROWS, HALF),
        buf(NY, 2 * Q_ROWS, HALF), buf(NY, 2 * Q_ROWS, HALF),
        buf(2 * Q_ROWS, WIDTH // 2), buf(NY, 2 * Q_ROWS, WIDTH // 2),
        buf(ND, GROUP, W_COLS),
        buf(CHUNKS, ND, GROUP, CHUNK), buf(CHUNKS, ND, GROUP, CHUNK),
        buf(HEADS, KEYS, WINDOW),
        buf(8, WINDOW, dtype=F32),
        buf(*rows, dtype=F32), buf(*rows, dtype=F32), buf(*rows, dtype=F32),
        buf(3, *rows, dtype=F32), buf(3, *rows, dtype=F32),
        buf(*rows, dtype=F32), buf(*rows, dtype=F32),
        buf(NY, K_ROWS, COLS), buf(NY, K_ROWS, COLS),
        buf(NZ, GROUP, COLS, dtype=F32), buf(NZ, W_ROWS, W_COLS, dtype=F32),
        buf(W_ROWS, W_COLS, dtype=F32),
        buf(16, GROUP, COLS), buf(16, GROUP, COLS),
        buf(HALF_Z, W_ROWS, W_COLS), buf(HALF_Z, W_ROWS, W_COLS),
        buf(HALF_Z, W_ROWS, W_COLS), buf(HALF_Z, W_ROWS, W_COLS),
        buf(NY, 2 * Q_ROWS, HALF), buf(NY, 2 * Q_ROWS, HALF),
        buf(Q_ROWS, WIDTH),
        dma((8, NY - 1)), dma((8, NY)),
        dma((2 + CHUNKS, ND - 1)), dma((2 + CHUNKS, ND)),
        dma((3, NZ)), dma((3, NZ)),
        dma((6,)), dma((6,)),
        dma((16,)), dma((16,)),
        dma((NZ,)), dma((NZ,)),
        dma((10,)),
    ]
    shapes = (
        jax.ShapeDtypeStruct((Q_ROWS, WIDTH), BF16),
        jax.ShapeDtypeStruct((K_ROWS, WIDTH), BF16),
        jax.ShapeDtypeStruct((K_ROWS, WIDTH), BF16),
        jax.ShapeDtypeStruct((W_ROWS, W_COLS), F32),
    )
    outs = pl.pallas_call(
        kernel,
        out_shape=shapes,
        in_specs=[pl.BlockSpec(memory_space=pltpu.HBM)] * 6 + [vmem, smem],
        out_specs=(hbm,) * 4,
        scratch_shapes=scratch,
        compiler_params=pltpu.CompilerParams(
            collective_id=0, has_side_effects=True, vmem_limit_bytes=VMEM_BYTES
        ),
        name="attention_backward",
    )(
        queries[0], saved_out[0], grad_out[0], key_vectors[0], value_vectors[0], out_weight,
        block_order.reshape(1, NY * NZ), window_start,
    )
    outs = pl.pallas_call(
        deliver,
        out_shape=shapes,
        in_specs=[hbm] * 4,
        out_specs=(hbm,) * 4,
        scratch_shapes=[pltpu.VMEM(shape.shape, shape.dtype) for shape in shapes] + [dma((2, 4))],
        compiler_params=pltpu.CompilerParams(vmem_limit_bytes=VMEM_BYTES),
        name="deliver",
    )(*outs)
    return (outs[0][None], outs[1][None], outs[2][None], outs[3])


def solution(mesh):
    rows = P("dp", "seq", None)
    return jax.shard_map(
        on_device,
        mesh=mesh,
        in_specs=(rows, rows, rows, rows, rows, P("seq", "dp"), P("dp"), P()),
        out_specs=(rows, rows, rows, P("seq", "dp")),
        check_vma=False,
    )
```

```python
import math

import jax
import jax.numpy as jnp
from jax import lax
from jax.experimental import pallas as pl
from jax.experimental.pallas import tpu as pltpu
from jax.sharding import PartitionSpec as P

HD = 128
NY, NZ, ND = 4, 16, 8
Q_ROWS = 8
K_ROWS = 128
WIDTH = 4096
COLS = WIDTH // NY
HEADS = COLS // HD
HALF = COLS // 2
GROUP = NY * Q_ROWS
WINDOW = NZ * GROUP
KEYS = NY * K_ROWS
W_ROWS = 64
W_COLS = WIDTH // ND
INV_ROOT = 1.0 / math.sqrt(HD)
LOG2E = 1.0 / math.log(2.0)
LOW = -1e30
HALF_Z = NZ // 2
CHUNKS = 4
CHUNK = COLS // CHUNKS
BLOCK = WINDOW // CHUNKS
PARTS = 2
PART_HEADS = HEADS // PARTS
SLOT = PART_HEADS * GROUP + 16
NEAR = 4
JUMP = 5
VMEM_BYTES = 64 * 1024 * 1024
BF16 = jnp.bfloat16
F32 = jnp.float32
MESH = pl.DeviceIdType.MESH


def dot_nt(a, b):
    return lax.dot_general(a, b, (((1,), (1,)), ((), ())), preferred_element_type=F32)


def dot_tn(a, b):
    return lax.dot_general(a, b, (((0,), (0,)), ((), ())), preferred_element_type=F32)


def dot_nn(a, b):
    return lax.dot_general(a, b, (((1,), (0,)), ((), ())), preferred_element_type=F32)


def fold(block):
    half = block.shape[1] // 2
    return jnp.concatenate([block[:, :half], block[:, half:]], 0)


def unfold(block):
    rows = block.shape[0] // 2
    return jnp.concatenate([block[:rows], block[rows:]], 1)


def kernel(
    q_ref, so_ref, go_ref, k_ref, v_ref, w_ref, order_ref, start_ref,
    gq_ref, gk_ref, gv_ref, gw_ref,
    q_own, so_own, go_own,
    kb, vb, qg, cg, wg, sog, gg,
    q_out, q_in, so_out, so_in, go_out, go_in, g_out,
    c_out, c_in, prob, query_pos, row_max, lse_own, lse_near, lse_a, lse_b, scale, delta,
    gvs, gks, dq, gwp, gw_out,
    dq_send, dq_recv, gw_sr, gw_sl, gw_rr, gw_rl, gq_out, gq_in, gq_all,
    y_send, y_recv, d_send, d_recv, ag_send, ag_recv, l_send, l_recv,
    dq_ssem, dq_rsem, gw_ssem, gw_rsem, local_sem,
):
    n = lax.axis_index("seq")
    s = lax.axis_index("dp")
    y = lax.div(n, NZ)
    z = lax.rem(n, NZ)

    def at_y(yy):
        return (yy * NZ + z, s)

    def at_d(ss):
        return (n, ss)

    def z_off(j):
        return lax.rem(z + (j + NZ), NZ)

    def at_z(j):
        return (y * NZ + z_off(j), s)

    y_peers = [lax.rem(y + j, NY) for j in range(1, NY)]
    d_peers = [lax.rem(s + j, ND) for j in range(1, ND)]
    z_low = lax.rem(z, 4)
    z_high = lax.div(z, 4)

    def nth_block(i):
        turn = i + lax.div(i, 2) - 2 * lax.div(i, 3)
        toward = 2 * lax.div(z_low, 2) - 1
        return lax.rem(z_high + 8 + toward * turn, CHUNKS)

    near = [(y * NZ + z - z_low + lax.rem(z_low + j, 4), s) for j in range(1, 4)]
    far = [at_z(4 * j) for j in range(1, 4)]

    barrier = pltpu.get_barrier_semaphore()
    peers = (
        [at_z(1), at_z(-1), at_z(JUMP), at_z(-JUMP)]
        + [at_y(p) for p in y_peers]
        + [at_d(p) for p in d_peers]
        + near
        + far
    )
    for p in peers:
        pl.semaphore_signal(barrier, inc=1, device_id=p, device_id_type=MESH)

    def cols_of(p):
        return pl.ds(pl.multiple_of(p * COLS, COLS), COLS)

    loads = [
        pltpu.make_async_copy(src, dst, local_sem.at[i])
        for i, (src, dst) in enumerate([
            (go_ref, go_own),
            (q_ref, q_own),
            (so_ref, so_own),
            (w_ref, wg.at[z]),
            (k_ref.at[:, cols_of(y)], kb.at[y]),
            (v_ref.at[:, cols_of(y)], vb.at[y]),
        ])
    ]
    for load in loads:
        load.start()

    row = lax.broadcasted_iota(jnp.int32, (NY * NZ, WINDOW), 0)
    place = lax.broadcasted_iota(jnp.int32, (NY * NZ, WINDOW), 1)
    holder = ((place >> 3) & (NY - 1)) * NZ + (place >> 5)
    select = jnp.where(row == holder, 1.0, 0.0).astype(BF16)
    order = jnp.broadcast_to(order_ref[...].astype(F32), (8, NY * NZ)).astype(BF16)
    inside = (lax.broadcasted_iota(jnp.int32, (8, WINDOW), 1) & (Q_ROWS - 1)).astype(F32)
    query_pos[...] = dot_nn(order, select) * Q_ROWS + inside + start_ref[0].astype(F32)

    loads[0].wait()
    go_out[...] = fold(go_own[...].astype(F32)).astype(BF16)
    loads[1].wait()
    loads[2].wait()
    q32 = q_own[...].astype(F32)
    so32 = so_own[...].astype(F32)
    for i in range(NY):
        q_out[i] = fold(q32[:, i * COLS : (i + 1) * COLS]).astype(BF16)
        so_out[i] = fold(so32[:, i * COLS : (i + 1) * COLS]).astype(BF16)
    go_in[pl.ds(y, 1)] = go_out[...][None]
    q_in[pl.ds(y, 1)] = q_out[pl.ds(y, 1)]
    so_in[pl.ds(y, 1)] = so_out[pl.ds(y, 1)]
    loads[3].wait()

    pl.semaphore_wait(barrier, len(peers))

    def remote(src, dst, send, recv, device):
        return pltpu.make_async_remote_copy(
            src_ref=src, dst_ref=dst, send_sem=send, recv_sem=recv,
            device_id=device, device_id_type=MESH,
        )

    streams = [wg, qg, cg.at[0], cg.at[1]]

    def z_send(stream, sem, distance, hop):
        buf, slot = streams[stream], z_off(-distance)
        return remote(
            buf.at[slot], buf.at[slot], ag_send.at[stream, sem], ag_recv.at[stream, slot], at_z(hop)
        )

    def z_arrived(stream, distance):
        z_send(stream, 0, distance, 1).wait_recv()

    z_sends = {}

    def z_go(stream, distance, hop):
        sem = z_sends.get(stream, 0)
        z_sends[stream] = sem + 1
        z_send(stream, sem, distance, hop).start()

    def ring_start(stream):
        z_go(stream, 0, 1)
        z_go(stream, 0, -1)

    def ring_step(stream, k):
        z_arrived(stream, k)
        if k < HALF_Z:
            z_go(stream, k, 1)
            z_arrived(stream, -k)
            if k < HALF_Z - 1:
                z_go(stream, -k, -1)

    def wave_start(stream):
        z_go(stream, 0, 1)
        z_go(stream, 0, -1)
        z_go(stream, 0, JUMP)
        z_go(stream, 0, -JUMP)

    def wave_near(stream, k):
        for sign in (1, -1):
            z_arrived(stream, sign * k)
            if k < NEAR:
                z_go(stream, sign * k, sign)

    def wave_far(stream, k):
        for sign, last in ((1, HALF_Z), (-1, HALF_Z - 1)):
            distance = NEAR + k
            if distance <= last:
                z_arrived(stream, sign * distance)
            if distance < last:
                z_go(stream, sign * distance, sign)

    def z_drain(stream):
        @pl.loop(0, z_sends[stream])
        def _(sem):
            z_send(stream, sem, 0, 1).wait_send()

    W, Q, C = 0, 1, (2, 3)

    def part_cols(p, part):
        return pl.ds(pl.multiple_of(p * COLS + part * HALF, HALF), HALF)

    kinds = [
        (lambda p: go_out, lambda p: go_in.at[p]),
        (lambda p: q_out.at[p], lambda p: q_in.at[p]),
        (lambda p: so_out.at[p], lambda p: so_in.at[p]),
        (lambda p: k_ref.at[:, cols_of(p)], lambda p: kb.at[p]),
        (lambda p: v_ref.at[:, cols_of(p)], lambda p: vb.at[p]),
        (lambda p: gvs.at[0, p], lambda p: gv_ref.at[:, part_cols(p, 0)]),
        (lambda p: gvs.at[1, p], lambda p: gv_ref.at[:, part_cols(p, 1)]),
        (lambda p: gks.at[0, p], lambda p: gk_ref.at[:, part_cols(p, 0)]),
        (lambda p: gks.at[1, p], lambda p: gk_ref.at[:, part_cols(p, 1)]),
        (lambda p: gq_out.at[0, p], lambda p: gq_in.at[0, p]),
        (lambda p: gq_out.at[1, p], lambda p: gq_in.at[1, p]),
    ]
    GV, GK, GQ = (5, 6), (7, 8), (9, 10)

    def y_copy(kind, j, slot):
        src_of, dst_of = kinds[kind]
        p = y_peers[j]
        return remote(
            src_of(p), dst_of(slot), y_send.at[kind, j], y_recv.at[kind, slot], at_y(p)
        )

    def y_start(kind):
        for j in range(NY - 1):
            y_copy(kind, j, y).start()

    def y_arrived(kind):
        for j in range(NY - 1):
            y_copy(kind, j, y_peers[j]).wait_recv()

    def y_drain(kind):
        for j in range(NY - 1):
            y_copy(kind, j, y).wait_send()

    d_sends = []

    def d_start(kind, src_of, buf):
        for j in range(ND - 1):
            p = d_peers[j]
            copy = remote(
                src_of(p), buf.at[s], d_send.at[kind, j], d_recv.at[kind, s], at_d(p)
            )
            copy.start()
            d_sends.append(copy)

    def d_arrived(kind, buf):
        for j in range(ND - 1):
            p = d_peers[j]
            remote(
                buf.at[p], buf.at[p], d_send.at[kind, j], d_recv.at[kind, p], at_d(p)
            ).wait_recv()

    def partial_context(i):
        block = wg[pl.ds(4 * nth_block(i), 4)].reshape(CHUNK, W_COLS)
        part = dot_nt(gg[...].reshape(ND * GROUP, W_COLS), block)
        c_out[i] = part.reshape(ND, GROUP, CHUNK).astype(BF16)
        c_in[i, pl.ds(s, 1)] = c_out[i, pl.ds(s, 1)]
        d_start(2 + i, lambda p: c_out.at[i, p], c_in.at[i])

    def gw_right(k):
        return remote(gw_sr.at[k], gw_rr.at[k], gw_ssem.at[k], gw_rsem.at[k], at_z(1))

    def gw_left(k):
        i = HALF_Z + k
        return remote(gw_sl.at[k], gw_rl.at[k], gw_ssem.at[i], gw_rsem.at[i], at_z(-1))

    def gw_step(k):
        mine = gwp[pl.ds(z_off(HALF_Z - k), 1)][0]
        if k > 0:
            gw_right(k - 1).wait_recv()
            mine = mine + gw_rr[k - 1].astype(F32)
        gw_sr[k] = mine.astype(BF16)
        gw_right(k).start()
        if k < HALF_Z - 1:
            mine = gwp[pl.ds(z_off(k + 1 - HALF_Z), 1)][0]
            if k > 0:
                gw_left(k - 1).wait_recv()
                mine = mine + gw_rl[k - 1].astype(F32)
            gw_sl[k] = mine.astype(BF16)
            gw_left(k).start()

    gw_store = pltpu.make_async_copy(gw_out, gw_ref, local_sem.at[6])

    def gw_end():
        gw_left(HALF_Z - 2).wait_recv()
        gw_right(HALF_Z - 1).wait_recv()
        total = (
            gwp[pl.ds(z, 1)][0]
            + gw_rr[HALF_Z - 1].astype(F32)
            + gw_rl[HALF_Z - 2].astype(F32)
        )
        gw_out[...] = total * (1.0 / (ND * WINDOW))
        gw_store.start()

    def softmax_head(h):
        lanes = pl.ds(pl.multiple_of(h * HD, HD), HD)
        query = qg[:, :, lanes].reshape(WINDOW, HD)
        key_place = lax.broadcasted_iota(jnp.int32, (K_ROWS, WINDOW), 0).astype(F32)
        scores = []
        for b in range(NY):
            raw = dot_nt(kb[b, :, lanes], query) * (INV_ROOT * LOG2E)
            first_key = ((b * NZ + z) * K_ROWS).astype(F32)
            seen = key_place <= query_pos[0:1, :] - first_key
            scores.append(jnp.where(seen, raw, LOW))
        top = jnp.max(scores[0], 0, keepdims=True)
        for b in range(1, NY):
            top = jnp.maximum(top, jnp.max(scores[b], 0, keepdims=True))
        total = jnp.zeros((1, WINDOW), F32)
        for b in range(NY):
            e = jnp.exp2(scores[b] - top)
            total = total + jnp.sum(e, 0, keepdims=True)
            prob[h, b * K_ROWS : (b + 1) * K_ROWS] = e.astype(BF16)
        row_max[pl.ds(h, 1), :] = top
        lse_own[pl.ds(h, 1), :] = top + jnp.log2(total)

    def lse_copy(level, j):
        src, dst = ((lse_own, lse_a), (lse_near, lse_b))[level]
        i = level * 3 + j
        return remote(src, dst.at[j], l_send.at[i], l_recv.at[i], (near, far)[level][j])

    def joined(first, others):
        most = first
        for o in others:
            most = jnp.maximum(most, o)
        total = jnp.exp2(first - most)
        for o in others:
            total = total + jnp.exp2(o - most)
        return most + jnp.log2(total)

    def lse_start():
        for j in range(3):
            lse_copy(0, j).start()

    def lse_next():
        for j in range(3):
            lse_copy(0, j).wait()
        lse_near[...] = joined(lse_own[...], [lse_a[j] for j in range(3)])
        for j in range(3):
            lse_copy(1, j).start()

    def lse_end():
        for j in range(3):
            lse_copy(1, j).wait()
        lse = joined(lse_near[...], [lse_b[j] for j in range(3)])
        scale[...] = jnp.exp2(row_max[...] - lse)

    lane = lax.broadcasted_iota(jnp.int32, (GROUP, HD), 1)
    lane_head = (lane & 3) + ((lane >> 3) & 1) * PART_HEADS

    def own_context(i, sums):
        d_arrived(2 + i, c_in.at[i])
        context = c_in[i, 0].astype(F32)
        for d in range(1, ND):
            context = context + c_in[i, d].astype(F32)
        context = context.astype(BF16)
        chunk = nth_block(i)
        lanes = pl.ds(pl.multiple_of(chunk * CHUNK, CHUNK), CHUNK)
        product = context.astype(F32) * sog[pl.ds(s, 1), :, lanes][0].astype(F32)
        part = pl.ds(lax.div(chunk, 2), 1)
        for j in range(CHUNK // HD):
            first = lax.rem(chunk, 2) * (CHUNK // HD * GROUP) + j * GROUP
            own = slice(j * HD, (j + 1) * HD)
            cg[part, pl.ds(z, 1), pl.ds(pl.multiple_of(first, GROUP), GROUP), :] = context[
                :, own
            ][None, None]
            one = jnp.sum(product[:, own], 1, keepdims=True)
            sums = jnp.where(lane_head == chunk * (CHUNK // HD) + j, one, sums)
        return sums

    def own_delta(sums):
        high = sums.astype(BF16).astype(F32)
        rest = jnp.where((lane & PART_HEADS) == 0, high, sums - high).astype(BF16)
        row = lax.broadcasted_iota(jnp.int32, (GROUP, HD), 0)
        place = jnp.where(lane == row + z_low * GROUP, 1.0, 0.0).astype(BF16)
        tiles = dot_tn(rest, place)
        for p in range(PARTS):
            tile = tiles[8 * p : 8 * p + 8]
            tile = jnp.concatenate([tile, jnp.zeros_like(tile)], 0)
            cg[p, pl.ds(z, 1), PART_HEADS * GROUP :, :] = tile.astype(BF16)[None]

    def halves(k):
        ring_step(C[0], k)
        ring_step(C[1], k)

    def projection_gradient(i):
        block = sog[:, :, i * CHUNK : (i + 1) * CHUNK].reshape(ND * GROUP, CHUNK)
        piece = dot_tn(block, gg[...].reshape(ND * GROUP, W_COLS))
        gwp[4 * i : 4 * i + 4] = piece.reshape(4, W_ROWS, W_COLS)

    ring_start(W)
    y_start(1)
    y_start(0)
    y_start(2)

    ring_step(W, 1)
    y_arrived(1)
    rows = [unfold(q_in[i].astype(F32)) for i in range(NY)]
    qg[pl.ds(z, 1)] = jnp.concatenate(rows, 0).astype(BF16)[None]
    ring_start(Q)
    ring_step(W, 2)
    y_arrived(0)
    for d in range(ND):
        top, off = d // (ND // 2), (d % (ND // 2)) * W_COLS
        piece = [
            go_in[i].astype(F32)[top * Q_ROWS : (top + 1) * Q_ROWS, off : off + W_COLS]
            for i in range(NY)
        ]
        g_out[d] = jnp.concatenate(piece, 0).astype(BF16)
    gg[pl.ds(s, 1)] = g_out[pl.ds(s, 1)]
    d_start(0, lambda p: g_out.at[p], gg)
    ring_step(Q, 1)
    ring_step(W, 3)
    y_arrived(2)
    rows = [unfold(so_in[i].astype(F32)) for i in range(NY)]
    sog[pl.ds(s, 1)] = jnp.concatenate(rows, 0).astype(BF16)[None]
    d_start(1, lambda p: sog.at[s], sog)

    y_start(3)
    y_start(4)
    ring_step(Q, 2)
    ring_step(W, 4)
    ring_step(Q, 3)
    ring_step(W, 5)
    d_arrived(0, gg)
    d_arrived(1, sog)
    projection_gradient(0)
    projection_gradient(1)
    partial_context(0)
    ring_step(Q, 4)
    ring_step(W, 6)
    projection_gradient(2)
    projection_gradient(3)
    gw_step(0)
    partial_context(1)
    ring_step(Q, 5)
    ring_step(W, 7)
    gw_step(1)
    partial_context(2)
    ring_step(Q, 6)
    ring_step(W, 8)
    partial_context(3)
    sums = jnp.zeros((GROUP, HD), F32)
    for i in range(3):
        sums = own_context(i, sums)
    ring_step(Q, 7)
    gw_step(2)
    sums = own_context(3, sums)
    own_delta(sums)
    ring_start(C[0])
    ring_start(C[1])
    ring_step(Q, HALF_Z)

    loads[4].wait()
    y_arrived(3)

    @pl.loop(0, HEADS, unroll=2)
    def _(h):
        softmax_head(h)

        @pl.when(h == PART_HEADS - 1)
        def _():
            halves(1)

    lse_start()
    halves(2)
    gw_step(3)
    halves(3)
    lse_next()
    halves(4)
    gw_step(4)
    halves(5)
    halves(6)
    gw_step(5)
    halves(7)
    lse_end()
    loads[5].wait()
    y_arrived(4)
    ring_step(C[0], 8)

    chains = [(1, HALF_Z, 4), (-1, HALF_Z - 1, 3), (1, NEAR, 4), (-1, NEAR, 4)]

    def dq_copy(part, c, k):
        sign, reach, length = chains[c]
        hop = sign * JUMP if reach > NEAR and k == length - 1 else sign
        i = 4 * c + k
        return remote(
            dq_send.at[part, i], dq_recv.at[part, i], dq_ssem.at[part, i], dq_rsem.at[part, i],
            at_z(hop),
        )

    def dq_step(part, k):
        for c, (sign, reach, length) in enumerate(chains):
            if k < length:
                mine = dq[part, pl.ds(z_off(sign * (reach - k)), 1)][0]
                if k > 0:
                    dq_copy(part, c, k - 1).wait_recv()
                    mine = mine + dq_recv[part, 4 * c + k - 1].astype(F32)
                dq_send[part, 4 * c + k] = mine.astype(BF16)
                dq_copy(part, c, k).start()

    def dq_end(part):
        total = dq[part, pl.ds(z, 1)][0]
        for c in (2, 3, 0, 1):
            last = chains[c][2] - 1
            dq_copy(part, c, last).wait_recv()
            total = total + dq_recv[part, 4 * c + last].astype(F32)
        total = total * INV_ROOT
        for i in range(NY):
            gq_out[part, i] = fold(total[i * Q_ROWS : (i + 1) * Q_ROWS]).astype(BF16)
        gq_in[part, pl.ds(y, 1)] = gq_out[part, pl.ds(y, 1)]
        y_start(GQ[part])

    own_stores = [
        pltpu.make_async_copy(
            src.at[part, y], dst.at[:, part_cols(y, part)], local_sem.at[7 + 2 * part + i]
        )
        for part in range(PARTS)
        for i, (src, dst) in enumerate([(gvs, gv_ref), (gks, gk_ref)])
    ]

    def gradients(part):
        for i in range(CHUNKS):
            tile = cg[part, 4 * i : 4 * i + 4, PART_HEADS * GROUP :, :].astype(F32)
            tile = tile[0] + tile[1] + tile[2] + tile[3]
            delta[part, :PART_HEADS, i * BLOCK : (i + 1) * BLOCK] = (
                tile[:PART_HEADS] + tile[PART_HEADS : 2 * PART_HEADS]
            )

        @pl.loop(0, PART_HEADS, unroll=2)
        def _(i):
            h = part * PART_HEADS + i
            own = pl.ds(pl.multiple_of(i * HD, HD), HD)
            lanes = pl.ds(pl.multiple_of(h * HD, HD), HD)
            query = qg[:, :, lanes].reshape(WINDOW, HD)
            head_rows = pl.ds(pl.multiple_of(i * GROUP, GROUP), GROUP)
            ctx = cg[part, :, head_rows, :].reshape(WINDOW, HD)
            attend = prob[h].astype(F32) * scale[pl.ds(h, 1), :]
            value_grad = dot_nn(attend.astype(BF16), ctx)
            dprob = dot_nt(vb[:, :, lanes].reshape(KEYS, HD), ctx)
            dscore = (attend * (dprob - delta[part, pl.ds(i, 1), :])).astype(BF16)
            key_grad = dot_nn(dscore, query) * INV_ROOT
            query_grad = dot_tn(dscore, kb[:, :, lanes].reshape(KEYS, HD))
            gvs[part, :, :, own] = value_grad.astype(BF16).reshape(NY, K_ROWS, HD)
            gks[part, :, :, own] = key_grad.astype(BF16).reshape(NY, K_ROWS, HD)
            dq[part, :, :, own] = query_grad.reshape(NZ, GROUP, HD)

        dq_step(part, 0)
        y_start(GV[part])
        y_start(GK[part])
        own_stores[2 * part].start()
        own_stores[2 * part + 1].start()

    gradients(0)
    gw_step(6)
    ring_step(C[1], 8)
    gradients(1)
    gw_step(7)
    dq_step(0, 1)
    z_drain(W)
    dq_step(1, 1)
    z_drain(Q)
    dq_step(0, 2)
    dq_step(1, 2)
    z_drain(C[0])
    z_drain(C[1])
    dq_step(0, 3)
    dq_step(1, 3)
    for copy in d_sends:
        copy.wait_send()
    for kind in range(5):
        y_drain(kind)
    dq_end(0)
    dq_end(1)
    gw_end()
    for k in range(HALF_Z):
        gw_right(k).wait_send()
    for k in range(HALF_Z - 1):
        gw_left(k).wait_send()
    for part in range(PARTS):
        for c, (_, _, length) in enumerate(chains):
            for k in range(length):
                dq_copy(part, c, k).wait_send()
    for part in range(PARTS):
        y_arrived(GQ[part])
        for i in range(NY):
            first = i * COLS + part * HALF
            gq_all[:, first : first + HALF] = unfold(gq_in[part, i].astype(F32)).astype(BF16)
    gq_store = pltpu.make_async_copy(gq_all, gq_ref, local_sem.at[11])
    gq_store.start()
    for kind in GV + GK:
        y_arrived(kind)
    for kind in GV + GK + GQ:
        y_drain(kind)
    for store in own_stores:
        store.wait()
    gw_store.wait()
    gq_store.wait()


def deliver(*refs):
    count = (len(refs) - 1) // 3
    sources, results, stages = (refs[i * count : (i + 1) * count] for i in range(3))
    sem = refs[-1]
    fetches = [
        pltpu.make_async_copy(sources[i], stages[i], sem.at[0, i]) for i in range(count)
    ]
    stores = [
        pltpu.make_async_copy(stages[i], results[i], sem.at[1, i]) for i in range(count)
    ]
    for fetch in fetches:
        fetch.start()
    for fetch, store in zip(fetches, stores):
        fetch.wait()
        store.start()
    for store in stores:
        store.wait()


def on_device(
    queries, key_vectors, value_vectors, saved_out, grad_out, out_weight, window_start, block_order
):
    vmem = pl.BlockSpec(memory_space=pltpu.VMEM)
    smem = pl.BlockSpec(memory_space=pltpu.SMEM)
    hbm = pl.BlockSpec(memory_space=pl.ANY)

    def buf(*shape, dtype=BF16):
        return pltpu.VMEM(shape, dtype)

    dma = pltpu.SemaphoreType.DMA
    rows = (HEADS, WINDOW)
    scratch = [
        buf(Q_ROWS, WIDTH), buf(Q_ROWS, WIDTH), buf(Q_ROWS, WIDTH),
        buf(NY, K_ROWS, COLS), buf(NY, K_ROWS, COLS),
        buf(NZ, GROUP, COLS), buf(PARTS, NZ, SLOT, HD), buf(NZ, W_ROWS, W_COLS),
        buf(ND, GROUP, COLS), buf(ND, GROUP, W_COLS),
        buf(NY, 2 * Q_ROWS, HALF), buf(NY, 2 * Q_ROWS, HALF),
        buf(NY, 2 * Q_ROWS, HALF), buf(NY, 2 * Q_ROWS, HALF),
        buf(2 * Q_ROWS, WIDTH // 2), buf(NY, 2 * Q_ROWS, WIDTH // 2),
        buf(ND, GROUP, W_COLS),
        buf(CHUNKS, ND, GROUP, CHUNK), buf(CHUNKS, ND, GROUP, CHUNK),
        buf(HEADS, KEYS, WINDOW),
        buf(8, WINDOW, dtype=F32),
        buf(*rows, dtype=F32), buf(*rows, dtype=F32), buf(*rows, dtype=F32),
        buf(3, *rows, dtype=F32), buf(3, *rows, dtype=F32),
        buf(*rows, dtype=F32), buf(PARTS, 8, WINDOW, dtype=F32),
        buf(PARTS, NY, K_ROWS, HALF), buf(PARTS, NY, K_ROWS, HALF),
        buf(PARTS, NZ, GROUP, HALF, dtype=F32), buf(NZ, W_ROWS, W_COLS, dtype=F32),
        buf(W_ROWS, W_COLS, dtype=F32),
        buf(PARTS, 16, GROUP, HALF), buf(PARTS, 16, GROUP, HALF),
        buf(HALF_Z, W_ROWS, W_COLS), buf(HALF_Z, W_ROWS, W_COLS),
        buf(HALF_Z, W_ROWS, W_COLS), buf(HALF_Z, W_ROWS, W_COLS),
        buf(PARTS, NY, 2 * Q_ROWS, HALF // 2), buf(PARTS, NY, 2 * Q_ROWS, HALF // 2),
        buf(Q_ROWS, WIDTH),
        dma((11, NY - 1)), dma((11, NY)),
        dma((2 + CHUNKS, ND - 1)), dma((2 + CHUNKS, ND)),
        dma((4, NZ)), dma((4, NZ)),
        dma((6,)), dma((6,)),
        dma((PARTS, 16)), dma((PARTS, 16)),
        dma((NZ,)), dma((NZ,)),
        dma((12,)),
    ]
    shapes = (
        jax.ShapeDtypeStruct((Q_ROWS, WIDTH), BF16),
        jax.ShapeDtypeStruct((K_ROWS, WIDTH), BF16),
        jax.ShapeDtypeStruct((K_ROWS, WIDTH), BF16),
        jax.ShapeDtypeStruct((W_ROWS, W_COLS), F32),
    )
    outs = pl.pallas_call(
        kernel,
        out_shape=shapes,
        in_specs=[pl.BlockSpec(memory_space=pltpu.HBM)] * 6 + [vmem, smem],
        out_specs=(hbm,) * 4,
        scratch_shapes=scratch,
        compiler_params=pltpu.CompilerParams(
            collective_id=0, has_side_effects=True, vmem_limit_bytes=VMEM_BYTES
        ),
        name="attention_backward",
    )(
        queries[0], saved_out[0], grad_out[0], key_vectors[0], value_vectors[0], out_weight,
        block_order.reshape(1, NY * NZ), window_start,
    )
    outs = pl.pallas_call(
        deliver,
        out_shape=shapes,
        in_specs=[hbm] * 4,
        out_specs=(hbm,) * 4,
        scratch_shapes=[pltpu.VMEM(shape.shape, shape.dtype) for shape in shapes] + [dma((2, 4))],
        compiler_params=pltpu.CompilerParams(vmem_limit_bytes=VMEM_BYTES),
        name="deliver",
    )(*outs)
    return (outs[0][None], outs[1][None], outs[2][None], outs[3])


def solution(mesh):
    rows = P("dp", "seq", None)
    return jax.shard_map(
        on_device,
        mesh=mesh,
        in_specs=(rows, rows, rows, rows, rows, P("seq", "dp"), P("dp"), P()),
        out_specs=(rows, rows, rows, P("seq", "dp")),
        check_vma=False,
    )
```

```python
import math

import jax
import jax.numpy as jnp
from jax import lax
from jax.experimental import pallas as pl
from jax.experimental.pallas import tpu as pltpu
from jax.sharding import PartitionSpec as P

HD = 128
NY, NZ, ND = 4, 16, 8
Q_ROWS = 8
K_ROWS = 128
WIDTH = 4096
COLS = WIDTH // NY
HEADS = COLS // HD
HALF = COLS // 2
GROUP = NY * Q_ROWS
WINDOW = NZ * GROUP
KEYS = NY * K_ROWS
W_ROWS = 64
W_COLS = WIDTH // ND
INV_ROOT = 1.0 / math.sqrt(HD)
LOG2E = 1.0 / math.log(2.0)
LOW = -1e30
HALF_Z = NZ // 2
CHUNKS = 4
CHUNK = COLS // CHUNKS
BLOCK = WINDOW // CHUNKS
PARTS = 2
PART_HEADS = HEADS // PARTS
SLOT = PART_HEADS * GROUP + 16
NEAR = 4
JUMP = 5
VMEM_BYTES = 64 * 1024 * 1024
BF16 = jnp.bfloat16
F32 = jnp.float32
MESH = pl.DeviceIdType.MESH


def dot_nt(a, b):
    return lax.dot_general(a, b, (((1,), (1,)), ((), ())), preferred_element_type=F32)


def dot_tn(a, b):
    return lax.dot_general(a, b, (((0,), (0,)), ((), ())), preferred_element_type=F32)


def dot_nn(a, b):
    return lax.dot_general(a, b, (((1,), (0,)), ((), ())), preferred_element_type=F32)


def fold(block):
    half = block.shape[1] // 2
    return jnp.concatenate([block[:, :half], block[:, half:]], 0)


def unfold(block):
    rows = block.shape[0] // 2
    return jnp.concatenate([block[:rows], block[rows:]], 1)


def kernel(
    q_ref, so_ref, go_ref, k_ref, v_ref, w_ref, order_ref, start_ref,
    gq_ref, gk_ref, gv_ref, gw_ref,
    q_own, so_own, go_own,
    kb, vb, qg, cg, wg, sog, gg,
    q_out, q_in, so_out, so_in, go_out, go_in, g_out,
    c_out, c_in, prob, query_pos, row_max, lse_own, lse_near, lse_a, lse_b, lse_all, scale, delta,
    gvs, gks, dq, gwp, gw_out,
    dq_send, dq_recv, gw_sr, gw_sl, gw_rr, gw_rl, gq_out, gq_in, gq_all,
    y_send, y_recv, d_send, d_recv, ag_send, ag_recv, l_send, l_recv,
    dq_ssem, dq_rsem, gw_ssem, gw_rsem, local_sem,
):
    n = lax.axis_index("seq")
    s = lax.axis_index("dp")
    y = lax.div(n, NZ)
    z = lax.rem(n, NZ)

    def at_y(yy):
        return (yy * NZ + z, s)

    def at_d(ss):
        return (n, ss)

    def z_off(j):
        return lax.rem(z + (j + NZ), NZ)

    def at_z(j):
        return (y * NZ + z_off(j), s)

    y_peers = [lax.rem(y + j, NY) for j in range(1, NY)]
    d_peers = [lax.rem(s + j, ND) for j in range(1, ND)]
    z_low = lax.rem(z, 4)
    z_high = lax.div(z, 4)

    def nth_block(i):
        turn = i + lax.div(i, 2) - 2 * lax.div(i, 3)
        toward = 2 * lax.div(z_low, 2) - 1
        return lax.rem(z_high + 8 + toward * turn, CHUNKS)

    near = [(y * NZ + z - z_low + lax.rem(z_low + j, 4), s) for j in range(1, 4)]
    far = [at_z(4 * j) for j in range(1, 4)]

    barrier = pltpu.get_barrier_semaphore()
    peers = (
        [at_z(1), at_z(-1), at_z(JUMP), at_z(-JUMP)]
        + [at_y(p) for p in y_peers]
        + [at_d(p) for p in d_peers]
        + near
        + far
    )
    for p in peers:
        pl.semaphore_signal(barrier, inc=1, device_id=p, device_id_type=MESH)

    def cols_of(p):
        return pl.ds(pl.multiple_of(p * COLS, COLS), COLS)

    loads = [
        pltpu.make_async_copy(src, dst, local_sem.at[i])
        for i, (src, dst) in enumerate([
            (go_ref, go_own),
            (q_ref, q_own),
            (so_ref, so_own),
            (w_ref, wg.at[z]),
            (k_ref.at[:, cols_of(y)], kb.at[y]),
            (v_ref.at[:, cols_of(y)], vb.at[y]),
        ])
    ]
    for load in loads:
        load.start()

    row = lax.broadcasted_iota(jnp.int32, (NY * NZ, WINDOW), 0)
    place = lax.broadcasted_iota(jnp.int32, (NY * NZ, WINDOW), 1)
    holder = ((place >> 3) & (NY - 1)) * NZ + (place >> 5)
    select = jnp.where(row == holder, 1.0, 0.0).astype(BF16)
    order = jnp.broadcast_to(order_ref[...].astype(F32), (8, NY * NZ)).astype(BF16)
    inside = (lax.broadcasted_iota(jnp.int32, (8, WINDOW), 1) & (Q_ROWS - 1)).astype(F32)
    query_pos[...] = dot_nn(order, select) * Q_ROWS + inside + start_ref[0].astype(F32)

    loads[0].wait()
    go_out[...] = fold(go_own[...].astype(F32)).astype(BF16)
    loads[1].wait()
    loads[2].wait()
    q32 = q_own[...].astype(F32)
    so32 = so_own[...].astype(F32)
    for i in range(NY):
        q_out[i] = fold(q32[:, i * COLS : (i + 1) * COLS]).astype(BF16)
        so_out[i] = fold(so32[:, i * COLS : (i + 1) * COLS]).astype(BF16)
    go_in[pl.ds(y, 1)] = go_out[...][None]
    q_in[pl.ds(y, 1)] = q_out[pl.ds(y, 1)]
    so_in[pl.ds(y, 1)] = so_out[pl.ds(y, 1)]
    loads[3].wait()

    pl.semaphore_wait(barrier, len(peers))

    def remote(src, dst, send, recv, device):
        return pltpu.make_async_remote_copy(
            src_ref=src, dst_ref=dst, send_sem=send, recv_sem=recv,
            device_id=device, device_id_type=MESH,
        )

    streams = [wg, qg, cg.at[0], cg.at[1]]

    def z_send(stream, sem, distance, hop):
        buf, slot = streams[stream], z_off(-distance)
        return remote(
            buf.at[slot], buf.at[slot], ag_send.at[stream, sem], ag_recv.at[stream, slot], at_z(hop)
        )

    def z_arrived(stream, distance):
        z_send(stream, 0, distance, 1).wait_recv()

    z_sends = {}

    def z_go(stream, distance, hop):
        sem = z_sends.get(stream, 0)
        z_sends[stream] = sem + 1
        z_send(stream, sem, distance, hop).start()

    def ring_start(stream):
        z_go(stream, 0, 1)
        z_go(stream, 0, -1)

    def ring_step(stream, k):
        z_arrived(stream, k)
        if k < HALF_Z:
            z_go(stream, k, 1)
            z_arrived(stream, -k)
            if k < HALF_Z - 1:
                z_go(stream, -k, -1)

    def wave_start(stream):
        z_go(stream, 0, 1)
        z_go(stream, 0, -1)
        z_go(stream, 0, JUMP)
        z_go(stream, 0, -JUMP)

    def wave_near(stream, k):
        for sign in (1, -1):
            z_arrived(stream, sign * k)
            if k < NEAR:
                z_go(stream, sign * k, sign)

    def wave_far(stream, k):
        for sign, last in ((1, HALF_Z), (-1, HALF_Z - 1)):
            distance = NEAR + k
            if distance <= last:
                z_arrived(stream, sign * distance)
            if distance < last:
                z_go(stream, sign * distance, sign)

    def z_drain(stream):
        @pl.loop(0, z_sends[stream])
        def _(sem):
            z_send(stream, sem, 0, 1).wait_send()

    W, Q, C = 0, 1, (2, 3)

    def part_cols(p, part):
        return pl.ds(pl.multiple_of(p * COLS + part * HALF, HALF), HALF)

    kinds = [
        (lambda p: go_out, lambda p: go_in.at[p]),
        (lambda p: q_out.at[p], lambda p: q_in.at[p]),
        (lambda p: so_out.at[p], lambda p: so_in.at[p]),
        (lambda p: k_ref.at[:, cols_of(p)], lambda p: kb.at[p]),
        (lambda p: v_ref.at[:, cols_of(p)], lambda p: vb.at[p]),
        (lambda p: gvs.at[0, p], lambda p: gv_ref.at[:, part_cols(p, 0)]),
        (lambda p: gvs.at[1, p], lambda p: gv_ref.at[:, part_cols(p, 1)]),
        (lambda p: gks.at[0, p], lambda p: gk_ref.at[:, part_cols(p, 0)]),
        (lambda p: gks.at[1, p], lambda p: gk_ref.at[:, part_cols(p, 1)]),
        (lambda p: gq_out.at[0, p], lambda p: gq_in.at[0, p]),
        (lambda p: gq_out.at[1, p], lambda p: gq_in.at[1, p]),
    ]
    GV, GK, GQ = (5, 6), (7, 8), (9, 10)

    def y_copy(kind, j, slot):
        src_of, dst_of = kinds[kind]
        p = y_peers[j]
        return remote(
            src_of(p), dst_of(slot), y_send.at[kind, j], y_recv.at[kind, slot], at_y(p)
        )

    def y_start(kind):
        for j in range(NY - 1):
            y_copy(kind, j, y).start()

    def y_arrived(kind):
        for j in range(NY - 1):
            y_copy(kind, j, y_peers[j]).wait_recv()

    def y_drain(kind):
        for j in range(NY - 1):
            y_copy(kind, j, y).wait_send()

    d_sends = []

    def d_start(kind, src_of, buf):
        for j in range(ND - 1):
            p = d_peers[j]
            copy = remote(
                src_of(p), buf.at[s], d_send.at[kind, j], d_recv.at[kind, s], at_d(p)
            )
            copy.start()
            d_sends.append(copy)

    def d_arrived(kind, buf):
        for j in range(ND - 1):
            p = d_peers[j]
            remote(
                buf.at[p], buf.at[p], d_send.at[kind, j], d_recv.at[kind, p], at_d(p)
            ).wait_recv()

    def partial_context(i):
        block = wg[pl.ds(4 * nth_block(i), 4)].reshape(CHUNK, W_COLS)
        part = dot_nt(gg[...].reshape(ND * GROUP, W_COLS), block)
        c_out[i] = part.reshape(ND, GROUP, CHUNK).astype(BF16)
        c_in[i, pl.ds(s, 1)] = c_out[i, pl.ds(s, 1)]
        d_start(2 + i, lambda p: c_out.at[i, p], c_in.at[i])

    def gw_right(k):
        return remote(gw_sr.at[k], gw_rr.at[k], gw_ssem.at[k], gw_rsem.at[k], at_z(1))

    def gw_left(k):
        i = HALF_Z + k
        return remote(gw_sl.at[k], gw_rl.at[k], gw_ssem.at[i], gw_rsem.at[i], at_z(-1))

    def gw_step(k):
        mine = gwp[pl.ds(z_off(HALF_Z - k), 1)][0]
        if k > 0:
            gw_right(k - 1).wait_recv()
            mine = mine + gw_rr[k - 1].astype(F32)
        gw_sr[k] = mine.astype(BF16)
        gw_right(k).start()
        if k < HALF_Z - 1:
            mine = gwp[pl.ds(z_off(k + 1 - HALF_Z), 1)][0]
            if k > 0:
                gw_left(k - 1).wait_recv()
                mine = mine + gw_rl[k - 1].astype(F32)
            gw_sl[k] = mine.astype(BF16)
            gw_left(k).start()

    gw_store = pltpu.make_async_copy(gw_out, gw_ref, local_sem.at[6])

    def gw_end():
        gw_left(HALF_Z - 2).wait_recv()
        gw_right(HALF_Z - 1).wait_recv()
        total = (
            gwp[pl.ds(z, 1)][0]
            + gw_rr[HALF_Z - 1].astype(F32)
            + gw_rl[HALF_Z - 2].astype(F32)
        )
        gw_out[...] = total * (1.0 / (ND * WINDOW))
        gw_store.start()

    def softmax_head(h):
        lanes = pl.ds(pl.multiple_of(h * HD, HD), HD)
        query = qg[:, :, lanes].reshape(WINDOW, HD)
        key_place = lax.broadcasted_iota(jnp.int32, (K_ROWS, WINDOW), 0).astype(F32)
        scores = []
        for b in range(NY):
            raw = dot_nt(kb[b, :, lanes], query) * (INV_ROOT * LOG2E)
            first_key = ((b * NZ + z) * K_ROWS).astype(F32)
            seen = key_place <= query_pos[0:1, :] - first_key
            scores.append(jnp.where(seen, raw, LOW))
        top = jnp.max(scores[0], 0, keepdims=True)
        for b in range(1, NY):
            top = jnp.maximum(top, jnp.max(scores[b], 0, keepdims=True))
        total = jnp.zeros((1, WINDOW), F32)
        for b in range(NY):
            e = jnp.exp2(scores[b] - top)
            total = total + jnp.sum(e, 0, keepdims=True)
            prob[h, b * K_ROWS : (b + 1) * K_ROWS] = e.astype(BF16)
        row_max[pl.ds(h, 1), :] = top
        lse_own[pl.ds(h, 1), :] = top + jnp.log2(total)

    def lane_block(i):
        return pl.ds(pl.multiple_of(i * BLOCK, BLOCK), BLOCK)

    def lse_copy(level, j):
        low = lax.rem(z_low + j + 1, 4)
        src, dst = (
            (lse_own.at[:, lane_block(low)], lse_a.at[j]),
            (lse_near, lse_b.at[j]),
            (lse_all.at[z_low], lse_all.at[z_low]),
        )[level]
        i = level * 3 + j
        return remote(
            src, dst, l_send.at[i], l_recv.at[i], (near, far, near)[level][j]
        )

    def joined(first, others):
        most = first
        for o in others:
            most = jnp.maximum(most, o)
        total = jnp.exp2(first - most)
        for o in others:
            total = total + jnp.exp2(o - most)
        return most + jnp.log2(total)

    def lse_start():
        for j in range(3):
            lse_copy(0, j).start()

    def lse_next():
        for j in range(3):
            lse_copy(0, j).wait()
        lse_near[...] = joined(lse_own[:, lane_block(z_low)], [lse_a[j] for j in range(3)])
        for j in range(3):
            lse_copy(1, j).start()

    def lse_last():
        for j in range(3):
            lse_copy(1, j).wait()
        lse_all[pl.ds(z_low, 1)] = joined(lse_near[...], [lse_b[j] for j in range(3)])[None]
        for j in range(3):
            lse_copy(2, j).start()

    def lse_end():
        for j in range(3):
            lse_copy(2, j).wait()
        lse = jnp.concatenate([lse_all[i] for i in range(4)], 1)
        scale[...] = jnp.exp2(row_max[...] - lse)

    lane = lax.broadcasted_iota(jnp.int32, (GROUP, HD), 1)
    lane_head = (lane & 3) + ((lane >> 3) & 1) * PART_HEADS

    def own_context(i, sums):
        d_arrived(2 + i, c_in.at[i])
        context = c_in[i, 0].astype(F32)
        for d in range(1, ND):
            context = context + c_in[i, d].astype(F32)
        context = context.astype(BF16)
        chunk = nth_block(i)
        lanes = pl.ds(pl.multiple_of(chunk * CHUNK, CHUNK), CHUNK)
        product = context.astype(F32) * sog[pl.ds(s, 1), :, lanes][0].astype(F32)
        part = pl.ds(lax.div(chunk, 2), 1)
        for j in range(CHUNK // HD):
            first = lax.rem(chunk, 2) * (CHUNK // HD * GROUP) + j * GROUP
            own = slice(j * HD, (j + 1) * HD)
            cg[part, pl.ds(z, 1), pl.ds(pl.multiple_of(first, GROUP), GROUP), :] = context[
                :, own
            ][None, None]
            one = jnp.sum(product[:, own], 1, keepdims=True)
            sums = jnp.where(lane_head == chunk * (CHUNK // HD) + j, one, sums)
        return sums

    def own_delta(sums):
        high = sums.astype(BF16).astype(F32)
        rest = jnp.where((lane & PART_HEADS) == 0, high, sums - high).astype(BF16)
        row = lax.broadcasted_iota(jnp.int32, (GROUP, HD), 0)
        place = jnp.where(lane == row + z_low * GROUP, 1.0, 0.0).astype(BF16)
        tiles = dot_tn(rest, place)
        for p in range(PARTS):
            tile = tiles[8 * p : 8 * p + 8]
            tile = jnp.concatenate([tile, jnp.zeros_like(tile)], 0)
            cg[p, pl.ds(z, 1), PART_HEADS * GROUP :, :] = tile.astype(BF16)[None]

    def halves(k):
        ring_step(C[0], k)
        ring_step(C[1], k)

    def projection_gradient(i):
        block = sog[:, :, i * CHUNK : (i + 1) * CHUNK].reshape(ND * GROUP, CHUNK)
        piece = dot_tn(block, gg[...].reshape(ND * GROUP, W_COLS))
        gwp[4 * i : 4 * i + 4] = piece.reshape(4, W_ROWS, W_COLS)

    ring_start(W)
    y_start(1)
    y_start(0)
    y_start(2)

    ring_step(W, 1)
    y_arrived(1)
    rows = [unfold(q_in[i].astype(F32)) for i in range(NY)]
    qg[pl.ds(z, 1)] = jnp.concatenate(rows, 0).astype(BF16)[None]
    ring_start(Q)
    ring_step(W, 2)
    y_arrived(0)
    for d in range(ND):
        top, off = d // (ND // 2), (d % (ND // 2)) * W_COLS
        piece = [
            go_in[i].astype(F32)[top * Q_ROWS : (top + 1) * Q_ROWS, off : off + W_COLS]
            for i in range(NY)
        ]
        g_out[d] = jnp.concatenate(piece, 0).astype(BF16)
    gg[pl.ds(s, 1)] = g_out[pl.ds(s, 1)]
    d_start(0, lambda p: g_out.at[p], gg)
    ring_step(Q, 1)
    ring_step(W, 3)
    y_arrived(2)
    rows = [unfold(so_in[i].astype(F32)) for i in range(NY)]
    sog[pl.ds(s, 1)] = jnp.concatenate(rows, 0).astype(BF16)[None]
    d_start(1, lambda p: sog.at[s], sog)

    y_start(3)
    y_start(4)
    ring_step(Q, 2)
    ring_step(W, 4)
    ring_step(Q, 3)
    ring_step(W, 5)
    d_arrived(0, gg)
    d_arrived(1, sog)
    projection_gradient(0)
    projection_gradient(1)
    partial_context(0)
    ring_step(Q, 4)
    ring_step(W, 6)
    projection_gradient(2)
    projection_gradient(3)
    gw_step(0)
    partial_context(1)
    ring_step(Q, 5)
    ring_step(W, 7)
    gw_step(1)
    partial_context(2)
    ring_step(Q, 6)
    ring_step(W, 8)
    partial_context(3)
    sums = jnp.zeros((GROUP, HD), F32)
    for i in range(3):
        sums = own_context(i, sums)
    ring_step(Q, 7)
    gw_step(2)
    sums = own_context(3, sums)
    own_delta(sums)
    ring_start(C[0])
    ring_start(C[1])
    ring_step(Q, HALF_Z)

    loads[4].wait()
    y_arrived(3)

    @pl.loop(0, HEADS, unroll=2)
    def _(h):
        softmax_head(h)

        for k in (1, 2):

            @pl.when(h == PART_HEADS * k - 3)
            def _():
                halves(k)

    lse_start()
    gw_step(3)
    halves(3)
    lse_next()
    halves(4)
    gw_step(4)
    halves(5)
    lse_last()
    halves(6)
    gw_step(5)
    halves(7)
    lse_end()
    loads[5].wait()
    y_arrived(4)
    ring_step(C[0], 8)

    chains = [(1, HALF_Z, 4), (-1, HALF_Z - 1, 3), (1, NEAR, 4), (-1, NEAR, 4)]

    def dq_copy(part, c, k):
        sign, reach, length = chains[c]
        hop = sign * JUMP if reach > NEAR and k == length - 1 else sign
        i = 4 * c + k
        return remote(
            dq_send.at[part, i], dq_recv.at[part, i], dq_ssem.at[part, i], dq_rsem.at[part, i],
            at_z(hop),
        )

    def dq_step(part, k):
        for c, (sign, reach, length) in enumerate(chains):
            if k < length:
                mine = dq[part, pl.ds(z_off(sign * (reach - k)), 1)][0]
                if k > 0:
                    dq_copy(part, c, k - 1).wait_recv()
                    mine = mine + dq_recv[part, 4 * c + k - 1].astype(F32)
                dq_send[part, 4 * c + k] = mine.astype(BF16)
                dq_copy(part, c, k).start()

    def dq_end(part):
        total = dq[part, pl.ds(z, 1)][0]
        for c in (2, 3, 0, 1):
            last = chains[c][2] - 1
            dq_copy(part, c, last).wait_recv()
            total = total + dq_recv[part, 4 * c + last].astype(F32)
        total = total * INV_ROOT
        for i in range(NY):
            gq_out[part, i] = fold(total[i * Q_ROWS : (i + 1) * Q_ROWS]).astype(BF16)
        gq_in[part, pl.ds(y, 1)] = gq_out[part, pl.ds(y, 1)]
        y_start(GQ[part])

    own_stores = [
        pltpu.make_async_copy(
            src.at[part, y], dst.at[:, part_cols(y, part)], local_sem.at[7 + 2 * part + i]
        )
        for part in range(PARTS)
        for i, (src, dst) in enumerate([(gvs, gv_ref), (gks, gk_ref)])
    ]

    def gradients(part):
        for i in range(CHUNKS):
            tile = cg[part, 4 * i : 4 * i + 4, PART_HEADS * GROUP :, :].astype(F32)
            tile = tile[0] + tile[1] + tile[2] + tile[3]
            delta[part, :PART_HEADS, i * BLOCK : (i + 1) * BLOCK] = (
                tile[:PART_HEADS] + tile[PART_HEADS : 2 * PART_HEADS]
            )

        @pl.loop(0, PART_HEADS, unroll=4)
        def _(i):
            h = part * PART_HEADS + i
            own = pl.ds(pl.multiple_of(i * HD, HD), HD)
            lanes = pl.ds(pl.multiple_of(h * HD, HD), HD)
            query = qg[:, :, lanes].reshape(WINDOW, HD)
            head_rows = pl.ds(pl.multiple_of(i * GROUP, GROUP), GROUP)
            ctx = cg[part, :, head_rows, :].reshape(WINDOW, HD)
            attend = prob[h].astype(F32) * scale[pl.ds(h, 1), :]
            value_grad = dot_nn(attend.astype(BF16), ctx)
            dprob = dot_nt(vb[:, :, lanes].reshape(KEYS, HD), ctx)
            dscore = (attend * (dprob - delta[part, pl.ds(i, 1), :])).astype(BF16)
            key_grad = dot_nn(dscore, query) * INV_ROOT
            query_grad = dot_tn(dscore, kb[:, :, lanes].reshape(KEYS, HD))
            gvs[part, :, :, own] = value_grad.astype(BF16).reshape(NY, K_ROWS, HD)
            gks[part, :, :, own] = key_grad.astype(BF16).reshape(NY, K_ROWS, HD)
            dq[part, :, :, own] = query_grad.reshape(NZ, GROUP, HD)

        dq_step(part, 0)
        y_start(GV[part])
        y_start(GK[part])
        own_stores[2 * part].start()
        own_stores[2 * part + 1].start()

    gradients(0)
    gw_step(6)
    ring_step(C[1], 8)
    gradients(1)
    gw_step(7)
    dq_step(0, 1)
    z_drain(W)
    dq_step(1, 1)
    z_drain(Q)
    dq_step(0, 2)
    dq_step(1, 2)
    z_drain(C[0])
    z_drain(C[1])
    dq_step(0, 3)
    dq_step(1, 3)
    for copy in d_sends:
        copy.wait_send()
    for kind in range(5):
        y_drain(kind)
    dq_end(0)
    dq_end(1)
    gw_end()
    for k in range(HALF_Z):
        gw_right(k).wait_send()
    for k in range(HALF_Z - 1):
        gw_left(k).wait_send()
    for part in range(PARTS):
        for c, (_, _, length) in enumerate(chains):
            for k in range(length):
                dq_copy(part, c, k).wait_send()
    for part in range(PARTS):
        y_arrived(GQ[part])
        for i in range(NY):
            first = i * COLS + part * HALF
            gq_all[:, first : first + HALF] = unfold(gq_in[part, i].astype(F32)).astype(BF16)
    gq_store = pltpu.make_async_copy(gq_all, gq_ref, local_sem.at[11])
    gq_store.start()
    for kind in GV + GK:
        y_arrived(kind)
    for kind in GV + GK + GQ:
        y_drain(kind)
    for store in own_stores:
        store.wait()
    gw_store.wait()
    gq_store.wait()


def deliver(*refs):
    count = (len(refs) - 1) // 3
    sem = refs[-1]
    fetches, stores = [], []
    for source, result, stage in zip(*(refs[i * count : (i + 1) * count] for i in range(3))):
        rows = source.shape[0]
        size = min(rows, 32)
        for first in range(0, rows, size):
            piece = pl.ds(first, size)
            n = len(fetches)
            fetches.append(
                pltpu.make_async_copy(source.at[piece], stage.at[piece], sem.at[0, n])
            )
            stores.append(
                pltpu.make_async_copy(stage.at[piece], result.at[piece], sem.at[1, n])
            )
    for fetch in fetches:
        fetch.start()
    for fetch, store in zip(fetches, stores):
        fetch.wait()
        store.start()
    for store in stores:
        store.wait()


def on_device(
    queries, key_vectors, value_vectors, saved_out, grad_out, out_weight, window_start, block_order
):
    vmem = pl.BlockSpec(memory_space=pltpu.VMEM)
    smem = pl.BlockSpec(memory_space=pltpu.SMEM)
    hbm = pl.BlockSpec(memory_space=pl.ANY)

    def buf(*shape, dtype=BF16):
        return pltpu.VMEM(shape, dtype)

    dma = pltpu.SemaphoreType.DMA
    rows = (HEADS, WINDOW)
    scratch = [
        buf(Q_ROWS, WIDTH), buf(Q_ROWS, WIDTH), buf(Q_ROWS, WIDTH),
        buf(NY, K_ROWS, COLS), buf(NY, K_ROWS, COLS),
        buf(NZ, GROUP, COLS), buf(PARTS, NZ, SLOT, HD), buf(NZ, W_ROWS, W_COLS),
        buf(ND, GROUP, COLS), buf(ND, GROUP, W_COLS),
        buf(NY, 2 * Q_ROWS, HALF), buf(NY, 2 * Q_ROWS, HALF),
        buf(NY, 2 * Q_ROWS, HALF), buf(NY, 2 * Q_ROWS, HALF),
        buf(2 * Q_ROWS, WIDTH // 2), buf(NY, 2 * Q_ROWS, WIDTH // 2),
        buf(ND, GROUP, W_COLS),
        buf(CHUNKS, ND, GROUP, CHUNK), buf(CHUNKS, ND, GROUP, CHUNK),
        buf(HEADS, KEYS, WINDOW),
        buf(8, WINDOW, dtype=F32),
        buf(*rows, dtype=F32), buf(*rows, dtype=F32), buf(HEADS, BLOCK, dtype=F32),
        buf(3, HEADS, BLOCK, dtype=F32), buf(3, HEADS, BLOCK, dtype=F32),
        buf(4, HEADS, BLOCK, dtype=F32),
        buf(*rows, dtype=F32), buf(PARTS, 8, WINDOW, dtype=F32),
        buf(PARTS, NY, K_ROWS, HALF), buf(PARTS, NY, K_ROWS, HALF),
        buf(PARTS, NZ, GROUP, HALF, dtype=F32), buf(NZ, W_ROWS, W_COLS, dtype=F32),
        buf(W_ROWS, W_COLS, dtype=F32),
        buf(PARTS, 16, GROUP, HALF), buf(PARTS, 16, GROUP, HALF),
        buf(HALF_Z, W_ROWS, W_COLS), buf(HALF_Z, W_ROWS, W_COLS),
        buf(HALF_Z, W_ROWS, W_COLS), buf(HALF_Z, W_ROWS, W_COLS),
        buf(PARTS, NY, 2 * Q_ROWS, HALF // 2), buf(PARTS, NY, 2 * Q_ROWS, HALF // 2),
        buf(Q_ROWS, WIDTH),
        dma((11, NY - 1)), dma((11, NY)),
        dma((2 + CHUNKS, ND - 1)), dma((2 + CHUNKS, ND)),
        dma((4, NZ)), dma((4, NZ)),
        dma((9,)), dma((9,)),
        dma((PARTS, 16)), dma((PARTS, 16)),
        dma((NZ,)), dma((NZ,)),
        dma((12,)),
    ]
    shapes = (
        jax.ShapeDtypeStruct((Q_ROWS, WIDTH), BF16),
        jax.ShapeDtypeStruct((K_ROWS, WIDTH), BF16),
        jax.ShapeDtypeStruct((K_ROWS, WIDTH), BF16),
        jax.ShapeDtypeStruct((W_ROWS, W_COLS), F32),
    )
    outs = pl.pallas_call(
        kernel,
        out_shape=shapes,
        in_specs=[pl.BlockSpec(memory_space=pltpu.HBM)] * 6 + [vmem, smem],
        out_specs=(hbm,) * 4,
        scratch_shapes=scratch,
        compiler_params=pltpu.CompilerParams(
            collective_id=0, has_side_effects=True, vmem_limit_bytes=VMEM_BYTES
        ),
        name="attention_backward",
    )(
        queries[0], saved_out[0], grad_out[0], key_vectors[0], value_vectors[0], out_weight,
        block_order.reshape(1, NY * NZ), window_start,
    )
    outs = pl.pallas_call(
        deliver,
        out_shape=shapes,
        in_specs=[hbm] * 4,
        out_specs=(hbm,) * 4,
        scratch_shapes=[pltpu.VMEM(shape.shape, shape.dtype) for shape in shapes] + [dma((2, 11))],
        compiler_params=pltpu.CompilerParams(vmem_limit_bytes=VMEM_BYTES),
        name="deliver",
    )(*outs)
    return (outs[0][None], outs[1][None], outs[2][None], outs[3])


def solution(mesh):
    rows = P("dp", "seq", None)
    return jax.shard_map(
        on_device,
        mesh=mesh,
        in_specs=(rows, rows, rows, rows, rows, P("seq", "dp"), P("dp"), P()),
        out_specs=(rows, rows, rows, P("seq", "dp")),
        check_vma=False,
    )
```
